32 devices in a mesh: dp: 8 (over z, y), mp: 4 (over x, core).
Axes of the slice: x: 2, y: 2, z: 4, core: 2. Of those that a mesh axis runs over, the one named last changes fastest.
Arguments:
- tokens: bfloat16 [16384, 1024], P(('dp', 'mp')), may hold values from -6 to 6
- lengths: int32 [16], P('dp'), may hold values from 256 to 1024, as said below
- norm1_gain: float32 [1024], replicated, may hold values from 0.5 to 1.5
- in_weight: bfloat16 [3, 1024, 1024], P(None, 'mp'), may hold values from -0.1875 to 0.1875
- conv_weight: bfloat16 [3, 1024], P(None, 'mp'), may hold values from -3.5 to 3.5
- out_weight: bfloat16 [1024, 1024], P('mp'), may hold values from -0.1875 to 0.1875
- norm2_gain: float32 [1024], replicated, may hold values from 0.5 to 1.5
- gate_weight: bfloat16 [4608, 1024], P('mp'), may hold values from -0.1875 to 0.1875
- up_weight: bfloat16 [4608, 1024], P('mp'), may hold values from -0.1875 to 0.1875
- down_weight: bfloat16 [4608, 1024], P('mp'), may hold values from -0.09375 to 0.09375
- cotangent: bfloat16 [16384, 1024], P(('dp', 'mp')), may hold values from -6 to 6
Outputs:
- block_out: bfloat16 [16384, 1024], P(('dp', 'mp'))
- tokens_grad: bfloat16 [16384, 1024], P(('dp', 'mp'))
- norm1_gain_grad: float32 [1024], replicated
- in_weight_grad: float32 [3, 1024, 1024], P(None, 'mp')
- conv_weight_grad: float32 [3, 1024], P(None, 'mp')
- out_weight_grad: float32 [1024, 1024], P('mp')
- norm2_gain_grad: float32 [1024], replicated
- gate_weight_grad: float32 [4608, 1024], P('mp')
- up_weight_grad: float32 [4608, 1024], P('mp')
- down_weight_grad: float32 [4608, 1024], P('mp')
The draws below stay inside these ranges and needn't reach their ends.
Inputs may be any that keep to these rules, and one draw needn't show every extreme that they name: `lengths`: slots of a sequence past its length are padding; some sequence has all 1024 tokens and some has 256.
All inputs are finite; a program needn't handle non-finite values.
Results may differ from the reference program's by a relative error of at most 0.018.
Values may be sent and summed in bfloat16 or wider, within the bound.
A program may use at most 320 MiB of HBM per device.

```python
import math
import jax
import jax.numpy as jnp
from jax import lax

D = 1024
FF = 4608
KER = 3
SEQ_LEN = 1024
SEQS = 16
TOKENS = 16384


def draw_lengths(key, part):
    key = jax.random.fold_in(key, 11)
    keys = jax.random.split(key, 3)
    shortest = max(SEQ_LEN // 4, 1)
    values = jax.random.randint(keys[0], (SEQS,), shortest, SEQ_LEN + 1, dtype=jnp.int32)
    full_at = jax.random.randint(keys[1], (), 0, SEQS, dtype=jnp.int32)
    short_at = (full_at + 1 + jax.random.randint(keys[2], (), 0, max(SEQS - 1, 1), dtype=jnp.int32)) % SEQS
    seq_slots = jnp.arange(SEQS, dtype=jnp.int32)
    values = jnp.where(seq_slots == full_at, SEQ_LEN, values)
    values = jnp.where(seq_slots == short_at, shortest, values)
    return values.astype(jnp.int32)


def levels(own_key, shape, cuts, least, top_value):
    def one(axis_at, shards_of):
        steps = jax.random.uniform(jax.random.fold_in(jax.random.fold_in(own_key, 6), axis_at), (shards_of,), jnp.float32, least / len(cuts), top_value / len(cuts))
        return jnp.repeat(jnp.exp(steps), shape[axis_at] // shards_of).reshape((-1,) + (1,) * (len(shape) - axis_at - 1))

    level = one(*cuts[0])
    for cut in cuts[1:]:
        level = level * one(*cut)
    return level


def centred(key, shape, scale, bound, pieces=(), kind=jnp.bfloat16):
    factor_of = levels(key, shape, pieces, -0.22, 0.18) if pieces else 1.0
    array = jax.random.normal(key, shape, jnp.float32) * scale * factor_of
    return jnp.minimum(jnp.maximum(array, -bound), bound).astype(kind)


def setup_inputs(seed: int = 0) -> dict:
    splits = jax.random.split(jax.random.key(seed), 12)
    tokens = centred(splits[0], (TOKENS, D), 1.0, 6.0, ((0, 32),))
    lengths = draw_lengths(jax.random.fold_in(splits[11], 71), 0)
    norm1_gain = jnp.clip(1.0 + 0.1 * jax.random.normal(splits[2], (D,), jnp.float32), 0.5, 1.5)
    in_weight = centred(splits[3], (KER, D, D), D ** -0.5, 0.1875, ((1, 4),))
    conv_weight = centred(splits[4], (KER, D), KER ** -0.5, 3.5, ((1, 4),))
    out_weight = centred(splits[5], (D, D), D ** -0.5, 0.1875, ((0, 4),))
    norm2_gain = jnp.clip(1.0 + 0.1 * jax.random.normal(splits[6], (D,), jnp.float32), 0.5, 1.5)
    gate_weight = centred(splits[7], (FF, D), D ** -0.5, 0.1875, ((0, 4),))
    up_weight = centred(splits[8], (FF, D), D ** -0.5, 0.1875, ((0, 4),))
    down_weight = centred(splits[9], (FF, D), FF ** -0.5, 0.09375, ((0, 4),))
    cotangent = centred(splits[10], (TOKENS, D), 1.0, 6.0, ((0, 32),))
    return {"tokens": tokens, "lengths": lengths, "norm1_gain": norm1_gain, "in_weight": in_weight, "conv_weight": conv_weight, "out_weight": out_weight, "norm2_gain": norm2_gain, "gate_weight": gate_weight, "up_weight": up_weight, "down_weight": down_weight, "cotangent": cotangent}


NORM_EPS = 1e-05
PRECISE = lax.Precision.HIGHEST

@jax.custom_vjp
def low(v):
    return lax.optimization_barrier(v.astype(jnp.bfloat16)).astype(jnp.float32)

@jax.custom_vjp
def low_back(v):
    return v

def low_keep(v):
    return (low(v), None)

def low_pass(kept, grad):
    return (grad,)

def back_keep(v):
    return (v, None)

def back_low(kept, grad):
    return (low(grad),)
low.defvjp(low_keep, low_pass)
low_back.defvjp(back_keep, back_low)

def rms_scale(row_data):
    return lax.rsqrt(lax.optimization_barrier(jnp.mean(row_data * row_data, axis=-1, keepdims=True)) + NORM_EPS)

def block_forward(params, row_data, pad_mask):
    norm1_gain, in_weight, conv_weight, out_weight, norm2_gain, gate_weight, up_weight, down_weight = params
    normed_one = low(pad_mask[..., None] * row_data * rms_scale(row_data) * norm1_gain)
    projected = low_back(jnp.einsum('gti,kci->kgtc', normed_one, in_weight, precision=PRECISE))
    mixed_bx = projected[0] * projected[2]
    seq_slots = row_data.shape[1]
    padded = jnp.pad(mixed_bx, ((0, 0), (2, 0), (0, 0)))
    convolved = conv_weight[0] * padded[:, 0:seq_slots] + conv_weight[1] * padded[:, 1:seq_slots + 1] + conv_weight[2] * padded[:, 2:]
    mixer_out = low(projected[1] * convolved)
    branch = low_back(jnp.einsum('gtc,cd->gtd', mixer_out, out_weight, precision=PRECISE))
    hidden = row_data + branch
    normed_two = low(hidden * rms_scale(hidden) * norm2_gain)
    gate_pre = low_back(jnp.einsum('gti,fi->gtf', normed_two, gate_weight, precision=PRECISE))
    up_pre = low_back(jnp.einsum('gti,fi->gtf', normed_two, up_weight, precision=PRECISE))
    activ = low(jax.nn.silu(gate_pre) * up_pre)
    return hidden + jnp.einsum('gtf,fd->gtd', activ, down_weight, precision=PRECISE)

def reference(tokens, lengths, norm1_gain, in_weight, conv_weight, out_weight, norm2_gain, gate_weight, up_weight, down_weight, cotangent):
    params = (norm1_gain.astype(jnp.float32), in_weight.astype(jnp.float32), conv_weight.astype(jnp.float32), out_weight.astype(jnp.float32), norm2_gain.astype(jnp.float32), gate_weight.astype(jnp.float32), up_weight.astype(jnp.float32), down_weight.astype(jnp.float32))
    seq_count = lengths.shape[0]
    group_size = math.gcd(seq_count, max(1, 4096 // SEQ_LEN))
    step_count = seq_count // group_size
    width = tokens.shape[1]
    row_groups = tokens.astype(jnp.float32).reshape(step_count, group_size, SEQ_LEN, width)
    grad_groups = cotangent.astype(jnp.float32).reshape(step_count, group_size, SEQ_LEN, width)
    places = jnp.arange(SEQ_LEN, dtype=jnp.int32)
    pad_masks = (places[None, :] < lengths[:, None]).astype(jnp.float32).reshape(step_count, group_size, SEQ_LEN)

    def visit_group(totals, scan_item):
        row_piece, grad_piece, mask_piece = scan_item

        def apply_block(param_set, row_set):
            return block_forward(param_set, row_set, mask_piece)
        result, pullback = jax.vjp(apply_block, params, row_piece)
        param_grads, row_grads = pullback(grad_piece)
        totals = jax.tree.map(lambda left, right: left + right, totals, param_grads)
        return (totals, (result, row_grads))
    zero_grads = jax.tree.map(jnp.zeros_like, params)
    totals, (results, row_grads) = lax.scan(visit_group, zero_grads, (row_groups, grad_groups, pad_masks))
    block_out = results.reshape(tokens.shape).astype(jnp.bfloat16)
    tokens_grad = row_grads.reshape(tokens.shape).astype(jnp.bfloat16)
    return (block_out, tokens_grad, totals[0], totals[1], totals[2], totals[3], totals[4], totals[5], totals[6], totals[7])
```

```python
import functools

import jax
import jax.numpy as jnp
from jax import lax
from jax.experimental import pallas as pl
from jax.experimental.pallas import tpu as pltpu
from jax.sharding import PartitionSpec as P

SEQ_LEN = 1024
NORM_EPS = 1e-05
F32 = jnp.float32
BF16 = jnp.bfloat16
MESH = pl.DeviceIdType.MESH
LANES = 128


def rms_scale(row_data):
    return lax.rsqrt(jnp.mean(row_data * row_data, axis=-1, keepdims=True) + NORM_EPS)


def rms_back(grad_scaled, row_data, scale_rows):
    inner_mean = jnp.mean(grad_scaled * row_data, axis=-1, keepdims=True)
    return scale_rows * grad_scaled - row_data * (scale_rows * scale_rows * scale_rows) * inner_mean


def dot(left, right, left_dim, right_dim):
    return lax.dot_general(
        left, right, (((left_dim,), (right_dim,)), ((), ())), preferred_element_type=F32
    )


def to_partner(values):
    count = lax.axis_size("mp")
    return lax.ppermute(values, "mp", [(i, i ^ 1) for i in range(count)])


def to_chip(values, ahead):
    count = lax.axis_size("mp")
    return lax.ppermute(values, "mp", [(i, (i + 2 * ahead) % count) for i in range(count)])


def gather_rows(own):
    chips = lax.axis_size("mp") // 2
    first = lax.axis_index("mp") % 2 == 0
    mine = [own] + [to_chip(own, chips - r) for r in range(1, chips)]
    blocks = []
    for block in mine:
        other = to_partner(block)
        blocks += [jnp.where(first, block, other), jnp.where(first, other, block)]
    return jnp.concatenate(blocks, axis=0)


def scatter_sum(partial, own_rows):
    chips = lax.axis_size("mp") // 2
    first = lax.axis_index("mp") % 2 == 0
    blocks = partial.reshape(chips, 2, own_rows, partial.shape[-1])
    sums = []
    for r in range(chips):
        theirs = to_partner(jnp.where(first, blocks[r, 1], blocks[r, 0]))
        mine = jnp.where(first, blocks[r, 0], blocks[r, 1])
        sums.append(mine.astype(F32) + theirs.astype(F32))
    total = sums[0]
    for r in range(1, chips):
        total = total + to_chip(sums[r].astype(BF16), r).astype(F32)
    return total


def ring_place(device, count):
    z, y = device // 2, device % 2
    return y * (count - 1 - z) + (1 - y) * z


def ring_device(place, count):
    back = place // (count // 2)
    return (1 - back) * 2 * place + back * (2 * (count - 1 - place) + 1)


def ring_sum(pieces):
    count = lax.axis_size("dp")
    order = [ring_device(i, count) for i in range(count)]
    place = ring_place(lax.axis_index("dp"), count)
    right = [(order[i], order[(i + 1) % count]) for i in range(count)]
    left = [(b, a) for a, b in right]

    def take(source, half, index):
        return lax.dynamic_index_in_dim(source, half * count + index, 0, keepdims=False)

    total = jnp.zeros(pieces.shape, BF16)
    moving = [take(pieces, 0, place), take(pieces, 1, place)]
    for step in range(1, count):
        moving = [lax.ppermute(moving[0], "dp", right), lax.ppermute(moving[1], "dp", left)]
        at = [(place - step + count) % count, (place + step) % count]
        moving = [
            (moving[h].astype(F32) + take(pieces, h, at[h]).astype(F32)).astype(BF16)
            for h in range(2)
        ]
    at = [(place + 1) % count, (place - 1 + count) % count]
    for h in range(2):
        total = lax.dynamic_update_index_in_dim(total, moving[h], h * count + at[h], 0)
    for step in range(1, count):
        moving = [lax.ppermute(moving[0], "dp", right), lax.ppermute(moving[1], "dp", left)]
        at = [(place + 1 - step + count) % count, (place - 1 + step) % count]
        for h in range(2):
            total = lax.dynamic_update_index_in_dim(total, moving[h], h * count + at[h], 0)
    return total


def sum_weights(parts):
    count = 2 * lax.axis_size("dp")
    stacked = jnp.concatenate(
        [part.astype(BF16).reshape(count, part.shape[0] // count, part.shape[1]) for part in parts],
        axis=1,
    )
    total = ring_sum(stacked)
    results = []
    at = 0
    for part in parts:
        rows = part.shape[0] // count
        results.append(total[:, at : at + rows].reshape(part.shape).astype(F32))
        at += rows
    return results


def butterfly(values, axis):
    count = lax.axis_size(axis)
    step = 1
    while step < count:
        values = values + lax.ppermute(values, axis, [(i, i ^ step) for i in range(count)])
        step *= 2
    return values


def block_by_ops(
    tokens,
    lengths,
    norm1_gain,
    in_weight,
    conv_weight,
    out_weight,
    norm2_gain,
    gate_weight,
    up_weight,
    down_weight,
    cotangent,
):
    own_rows, width = tokens.shape
    chips = lax.axis_size("mp") // 2
    chip = lax.axis_index("mp") // 2
    core = lax.axis_index("mp") % 2
    positions = core * own_rows + jnp.arange(own_rows, dtype=jnp.int32)
    seq_slots = jnp.arange(lengths.shape[0], dtype=jnp.int32)
    own_length = jnp.sum(jnp.where(seq_slots == chip, lengths, 0))
    own_mask = (positions < own_length).astype(F32)[:, None]
    channels = in_weight.shape[1]
    group_rows = 2 * chips * own_rows
    x_rows = tokens.astype(F32)
    scale_one = rms_scale(x_rows)
    normed_one = (own_mask * x_rows * scale_one * norm1_gain).astype(BF16)
    normed_one_all = gather_rows(normed_one)
    proj, shifted, conv, mixer_out = mixer_forward(normed_one_all, in_weight, conv_weight, chips)
    branch = scatter_sum(dot(mixer_out, out_weight, 1, 0).astype(BF16), own_rows)
    hidden = x_rows + branch
    scale_two = rms_scale(hidden)
    normed_two = (hidden * scale_two * norm2_gain).astype(BF16)
    normed_two_all = gather_rows(normed_two)
    cot_all = gather_rows(cotangent)
    gate_pre = dot(normed_two_all, gate_weight, 1, 1)
    up_pre = dot(normed_two_all, up_weight, 1, 1)
    squash = jax.nn.sigmoid(gate_pre)
    activ = (gate_pre * squash * up_pre).astype(BF16)
    grad_activ = dot(cot_all, down_weight, 1, 1)
    grad_gate = (grad_activ * up_pre * squash * (1.0 + gate_pre * (1.0 - squash))).astype(BF16)
    grad_up = (grad_activ * gate_pre * squash).astype(BF16)
    down_grad = dot(activ, cot_all, 0, 0)
    gate_grad = dot(grad_gate, normed_two_all, 0, 0)
    up_grad = dot(grad_up, normed_two_all, 0, 0)
    down_grad, gate_grad, up_grad = sum_weights([down_grad, gate_grad, up_grad])

    grad_normed_two = scatter_sum(
        (dot(grad_gate, gate_weight, 1, 0) + dot(grad_up, up_weight, 1, 0)).astype(BF16), own_rows
    )
    gain_two = jnp.sum(grad_normed_two * hidden * scale_two, axis=0)
    grad_hidden = cotangent.astype(F32) + rms_back(grad_normed_two * norm2_gain, hidden, scale_two)
    branch_all = gather_rows(grad_hidden.astype(BF16))
    taps = conv_weight.astype(F32)
    out_grad = dot(mixer_out, branch_all, 0, 0)
    grad_mixer = dot(branch_all, out_weight, 1, 1).reshape(chips, 2 * own_rows, channels)
    grad_conv = grad_mixer * proj[1]
    conv_grad = jnp.stack([jnp.sum(grad_conv * shifted[k], axis=(0, 1)) for k in range(3)])
    grad_pad = jnp.pad(grad_conv, ((0, 0), (0, 2), (0, 0)))
    grad_mixed = (
        taps[2] * grad_conv
        + taps[1] * grad_pad[:, 1 : 1 + 2 * own_rows]
        + taps[0] * grad_pad[:, 2 : 2 + 2 * own_rows]
    )
    grad_proj = [
        piece.astype(BF16).reshape(group_rows, channels)
        for piece in (grad_mixed * proj[2], grad_mixer * conv, grad_mixed * proj[0])
    ]
    in_grad = [dot(piece, normed_one_all, 0, 0) for piece in grad_proj]
    in_grad_0, in_grad_1, in_grad_2, out_grad = sum_weights(in_grad + [out_grad])
    grad_normed_one = scatter_sum(
        sum(dot(grad_proj[k], in_weight[k], 1, 0) for k in range(3)).astype(BF16), own_rows
    )
    masked_grad = own_mask * grad_normed_one
    gain_one = jnp.sum(masked_grad * x_rows * scale_one, axis=0)
    grad_tokens = grad_hidden + rms_back(masked_grad * norm1_gain, x_rows, scale_one)
    gains = butterfly(jnp.concatenate([gain_one, gain_two]), "mp")
    small = butterfly(jnp.concatenate([gains, conv_grad.reshape(-1)]), "dp")
    result = hidden + scatter_sum(dot(activ, down_weight, 1, 0).astype(BF16), own_rows)
    return (
        result.astype(BF16),
        grad_tokens.astype(BF16),
        small[:width],
        jnp.stack([in_grad_0, in_grad_1, in_grad_2]),
        small[2 * width :].reshape(3, channels),
        out_grad,
        small[width : 2 * width],
        gate_grad,
        up_grad,
        down_grad,
    )


def mixer_forward(normed_one_all, in_weight, conv_weight, chips):
    rows = normed_one_all.shape[0] // chips
    channels = in_weight.shape[1]
    proj = [dot(normed_one_all, in_weight[k], 1, 1).reshape(chips, rows, channels) for k in range(3)]
    taps = conv_weight.astype(F32)
    mixed_pad = jnp.pad(proj[0] * proj[2], ((0, 0), (2, 0), (0, 0)))
    shifted = [mixed_pad[:, k : k + rows] for k in range(3)]
    conv = taps[0] * shifted[0] + taps[1] * shifted[1] + taps[2] * shifted[2]
    mixer_out = (proj[1] * conv).astype(BF16).reshape(chips * rows, channels)
    return proj, shifted, conv, mixer_out


CHUNKS = 3
TILE = 256
KINDS = (
    ("A1", "PF1", "PF2", "PF3", "PG1", "PG2", "PG3")
    + ("QF1", "QF2", "QF3", "QSW", "QG1", "QG2", "QG3")
)
AT_END = (
    (),
    (),
    (0,),
    (100,),
    (),
    (9,),
    (200,),
    (109, 300),
    (3, 10),
    (110, 209),
    (),
    (309, 103),
    (210, 203),
    (),
    (),
    (303, 400, 6),
    (),
    (500, 13),
    (310,),
    (113,),
    (409, 509),
    (),
    (),
    (106,),
    (410, 213, 510),
    (206,),
    (),
    (306,),
    (),
    (403,),
    (),
    (),
    (600, 503),
    (313,),
    (700,),
    (800, 413),
    (900, 513, 609, 709, 809, 610, 909, 710, 603, 810, 406, 910, 703),
    (803, 903, 506, 613),
    (),
    (713,),
    (),
    (606,),
    (813, 913, 706, 806, 906),
)
INSIDE = (
    (),
    (7,),
    (0, 107, 8, 100),
    (),
    (1,),
    (108, 207),
    (200, 2, 307),
    (208, 101, 300, 201),
    (308, 301, 102),
    (4, 202, 11, 302),
    (111,),
    (5, 407),
    (12, 507),
    (),
    (),
    (400, 112, 104, 408),
    (211, 500, 204),
    (508,),
    (304, 105),
    (401,),
    (212, 501, 205, 311),
    (),
    (),
    (305, 402),
    (502, 312, 411),
    (),
    (),
    (511,),
    (412,),
    (607, 707),
    (807, 600, 512),
    (),
    (907, 608, 700, 708),
    (808, 601, 800, 908),
    (404,),
    (900, 602, 701, 504),
    (801, 405, 901, 702, 505, 611, 802, 711, 902, 604, 612, 811, 712, 911, 605, 704, 812),
    (912, 705, 804, 904),
    (),
    (),
    (805,),
    (905,),
    (),
)
CUT = 2
SLABS = 4
STRIP = 128
EDGE = 8


def block_kernel(
    count,
    tok_hbm,
    cot_hbm,
    gate_hbm,
    up_hbm,
    down_hbm,
    inw_hbm,
    outw_hbm,
    conv_ref,
    gain1,
    gain2,
    lengths,
    out_hbm,
    tg_hbm,
    gate_out,
    up_out,
    down_out,
    in_out,
    mix_out,
    small_out,
    n1_hbm,
    acts,
    wgu,
    wd,
    agu,
    aa,
    gf,
    land_a,
    land_p,
    land_q,
    gm,
    sa,
    ra,
    xr,
    wmix,
    f1,
    f2,
    taps,
    taps2,
    mbuf,
    gbuf,
    pbuf,
    smv,
    smb,
    ld_sem,
    ring_send,
    ring_recv,
    sum_send,
    sum_recv,
    half_free,
    rows_free,
    slots_free,
    mp_send,
    mp_recv,
    credit,
):
    own, width = out_hbm.shape
    group = 4 * own
    hidden_units = wd.shape[0]
    chunk = hidden_units // CHUNKS
    channels = outw_hbm.shape[0]
    per_block = own // TILE

    me_dp, me_mp = lax.axis_index("dp"), lax.axis_index("mp")
    core = me_mp % 2
    partner = (me_dp, me_mp + 1 - 2 * core)
    across = (me_dp, (me_mp + 2) % 4)
    place = ring_place(me_dp, count)
    nexts = [
        (ring_device((place + step) % count, count), me_mp) for step in (1, count - 1)
    ]
    signs = (1, -1)
    z, y = me_dp // 2, me_dp % 2
    side = z // 2
    inside = ((z + 1) // 2) % 2 == 1
    beside = (2 * z + 1 - y, me_mp)
    along = (2 * (z + 1 - 2 * (z % 2)) + y, me_mp)
    middle = (2 * (3 - z) + y, me_mp)
    opposite = (2 * ((z + 2) % 4) + y, me_mp)

    def rows_at(r, c):
        return pl.multiple_of((2 * r + c) * own, own)

    mine, theirs = core, 1 - core

    def load(src, dst, index):
        return pltpu.make_async_copy(src, dst, ld_sem.at[index])

    def weight_loads(c):
        at = pl.multiple_of(c * chunk, chunk)
        to = pl.multiple_of(2 * c * chunk, chunk)
        rows = pl.ds(at, chunk)
        return [
            load(gate_hbm.at[rows], wgu.at[pl.ds(to, chunk)], 3 * c),
            load(up_hbm.at[rows], wgu.at[pl.ds(to + chunk, chunk)], 3 * c + 1),
            load(down_hbm.at[rows], wd.at[rows], 3 * c + 2),
        ]

    def block_of(ref, r, c):
        return ref.at[pl.ds(rows_at(r, c), own)]

    inw = wmix.at[pl.ds(0, 3 * channels)]
    outw = wmix.at[pl.ds(3 * channels, channels)]
    late = 3 * CHUNKS
    inw_load = load(inw_hbm, inw, late)
    outw_load = load(outw_hbm, outw, late + 1)
    tok_load = load(tok_hbm, ra.at[1], late + 2)
    tok_again = load(tok_hbm, acts.at[0, pl.ds(0, own)], late + 2)
    cot_load = load(cot_hbm, block_of(acts.at[1], 0, mine), late + 3)
    n1_load = load(n1_hbm, acts.at[0, pl.ds(0, 2 * own)], late + 4)
    n1_move = load(gm.at[pl.ds(0, 2 * own)], acts.at[0, pl.ds(2 * own, 2 * own)], late + 9)
    out_store = load(sa.at[0], out_hbm, late + 5)
    tg_store = load(sa.at[1], tg_hbm, late + 6)
    n1_stores = [
        load(sa.at[c], n1_hbm.at[pl.ds(c * own, own)], late + 7 + c) for c in range(2)
    ]
    late += 10
    grad_stores = [
        load(
            gf.at[c, pl.ds(k * chunk, chunk)],
            ref.at[pl.ds(c * chunk, chunk)],
            late + CHUNKS * k + c,
        )
        for k, ref in enumerate((gate_out, up_out, down_out))
        for c in range(CHUNKS)
    ]
    late += 3 * CHUNKS
    mixer_stores = [
        load(gm.at[pl.ds(0, 3 * channels)], in_out, late),
        load(gm.at[pl.ds(3 * channels, channels)], mix_out, late + 1),
    ]

    for item in (inw_load, outw_load, cot_load, tok_load):
        item.start()
    for c in range(CHUNKS):
        for item in weight_loads(c):
            item.start()

    barrier = pltpu.get_barrier_semaphore()
    for device in (partner, across, beside, along, opposite):
        pl.semaphore_signal(barrier, inc=1, device_id=device, device_id_type=MESH)

    @pl.when(inside)
    def _():
        pl.semaphore_signal(barrier, inc=1, device_id=middle, device_id_type=MESH)
        pl.semaphore_wait(barrier, 6)

    @pl.when(jnp.logical_not(inside))
    def _():
        pl.semaphore_wait(barrier, 5)

    def ring_copy(src, dst, lane, h, number):
        return pltpu.make_async_remote_copy(
            src_ref=src,
            dst_ref=dst,
            send_sem=ring_send.at[lane, h, number],
            recv_sem=ring_recv.at[lane, h, number],
            device_id=nexts[h],
            device_id_type=MESH,
        )

    first = 5 * width // 8

    def make_part(bucket, start, rows, landing, number):
        quarter, two = rows // 4, rows // 2

        def own_half(h):
            at = pl.multiple_of(start + h * two, 16)
            return bucket.at[pl.ds(at, two), pl.ds(0, first)]

        def part_p(f):
            at = pl.multiple_of(start + y * two + f * quarter, 16)
            return bucket.at[pl.ds(at, quarter), pl.ds(0, first)]

        def part_q(f):
            at = pl.multiple_of(start + f * two, 16)
            return bucket.at[pl.ds(at, two), pl.ds(first, width - first)]

        def send(index, src, dst, device):
            return pltpu.make_async_remote_copy(
                src_ref=src,
                dst_ref=dst,
                send_sem=sum_send.at[number, index],
                recv_sem=sum_recv.at[number, index],
                device_id=device,
                device_id_type=MESH,
            )

        def arrived(index, ref):
            send(index, ref, ref, beside).wait_recv()

        def sent(index, ref):
            send(index, ref, ref, beside).wait_send()

        def add(target, ref):
            target[...] = target[...] + ref[...]

        land_a, land_p, land_q = landing
        ours, other = side, 1 - side
        a1, p1, p2, q1, q2, pg1, pg2, qg1, qg2, ya, yb = range(11)

        def half_sum(f):
            return land_a.at[pl.ds(pl.multiple_of(f * quarter, 16), quarter)]

        def begin():
            send(a1, own_half(1 - y), land_a, beside).start()

            @pl.when(jnp.logical_not(inside))
            def _():
                send(q1, part_q(ours), land_q[0], along).start()

        told = set()

        def hand_over(index, f, at_end):
            if at_end not in told:
                told.add(at_end)
                pl.semaphore_wait(half_free.at[number], 1)
            send(index, part_p(f), part_p(f), beside).start()

        def sum_rows(kind, at_end):
            if kind == "A1":
                arrived(a1, land_a)
                add(land_a, own_half(y))
                if at_end:
                    send(p1, half_sum(ours), land_p[0], along).start()
                sent(a1, land_a)
                pl.semaphore_signal(
                    half_free.at[number], inc=1, device_id=beside, device_id_type=MESH
                )
            elif kind == "PF1":
                arrived(p1, land_p[0])
                add(land_p[0], half_sum(ours))
                send(p2, land_p[0], land_p[1], middle).start()
            elif kind == "PF2":
                arrived(p2, land_p[1])
                add(land_p[1], half_sum(other))
                send(p1, land_p[1], land_p[0], along).start()
            elif kind == "PF3":
                arrived(p1, land_p[0])
                part_p(other)[...] = land_p[0][...] + half_sum(other)[...]
                send(pg1, part_p(other), part_p(other), along).start()
                hand_over(ya, other, at_end)
            elif kind == "PG1":
                arrived(pg1, part_p(other))
                send(pg2, part_p(other), part_p(other), middle).start()
                hand_over(ya, other, at_end)
            elif kind == "PG2":
                arrived(pg2, part_p(ours))
                send(pg1, part_p(ours), part_p(ours), along).start()
                hand_over(yb, ours, at_end)
            elif kind == "PG3":
                arrived(pg1, part_p(ours))
                hand_over(yb, ours, at_end)
            elif kind == "QF1":
                arrived(q1, land_q[0])
                add(land_q[0], part_q(ours))
                send(q2, land_q[0], land_q[1], middle).start()
            elif kind == "QF2":
                arrived(q2, land_q[1])
                add(land_q[1], part_q(other))
                send(q1, land_q[1], land_q[0], along).start()
            elif kind == "QF3":
                arrived(q1, land_q[0])
                add(land_q[0], part_q(other))
                send(q2, land_q[0], land_q[1], beside).start()
                sent(q1, land_q[0])
                pl.semaphore_signal(
                    rows_free.at[number], inc=1, device_id=along, device_id_type=MESH
                )
            elif kind == "QSW":
                arrived(q2, land_q[1])
                part_q(other)[...] = land_q[0][...] + land_q[1][...]
                send(qg1, part_q(other), part_q(other), along).start()
            elif kind == "QG1":
                arrived(qg1, part_q(other))
                send(qg2, part_q(other), part_q(other), middle).start()
            elif kind == "QG2":
                arrived(qg2, part_q(ours))
                pl.semaphore_wait(rows_free.at[number], 1)
                send(qg1, part_q(ours), part_q(ours), along).start()
            elif kind == "QG3":
                arrived(qg1, part_q(ours))

        def end():
            for index, f in ((ya, other), (yb, ours)):
                at = pl.multiple_of(start + (1 - y) * two + f * quarter, 16)
                arrived(index, bucket.at[pl.ds(at, quarter), pl.ds(0, first)])
            for index in (p1, pg1, ya, yb):
                sent(index, part_p(0))
            for index in (q2, qg1):
                sent(index, part_q(0))

            @pl.when(inside)
            def _():
                for index in (p2, pg2):
                    sent(index, part_p(0))
                for index in (q1, qg2):
                    sent(index, part_q(0))

        return begin, sum_rows, end

    part_rows, slab_rows = 3 * chunk // CUT, 4 * channels // SLABS
    parts_list = []
    for c in range(CHUNKS):
        for k in range(CUT):
            slot = CUT * c + k
            landing = (
                land_a.at[slot],
                [land_p.at[slot, 0], land_p.at[slot, 1]],
                [land_q.at[slot, 0], land_q.at[slot, 1]],
            )
            parts_list.append(make_part(gf.at[c], k * part_rows, part_rows, landing, slot))
    for k in range(SLABS):
        slot, upper = k // 2, k % 2
        two, quarter = slab_rows // 2, slab_rows // 4
        landing = (
            land_a.at[slot, pl.ds(upper * two, two)],
            [land_p.at[slot, i, pl.ds(upper * quarter, quarter)] for i in range(2)],
            [land_q.at[slot, i, pl.ds(upper * two, two)] for i in range(2)],
        )
        parts_list.append(
            make_part(gm, k * slab_rows, slab_rows, landing, CUT * CHUNKS + k)
        )

    def sum_start(c):
        chosen = range(CUT * c, CUT * c + CUT) if c < CHUNKS else range(CUT * c, len(parts_list))
        for number in chosen:
            parts_list[number][0]()

    def chunk_end(c):
        for number in range(CUT * c, CUT * c + CUT):
            parts_list[number][2]()
        for item in grad_stores[c::CHUNKS]:
            item.start()

    sites = iter(zip(AT_END, INSIDE))

    def pump():
        at_end, within = next(sites)

        @pl.when(jnp.logical_not(inside))
        def _():
            for event in at_end:
                parts_list[event // 100][1](KINDS[event % 100], True)

        @pl.when(inside)
        def _():
            for event in within:
                parts_list[event // 100][1](KINDS[event % 100], False)

    def mp_copy(src, dst, device, number):
        return pltpu.make_async_remote_copy(
            src_ref=src,
            dst_ref=dst,
            send_sem=mp_send.at[number],
            recv_sem=mp_recv.at[number],
            device_id=device,
            device_id_type=MESH,
        )

    def block_tiles(r, c, body):
        @pl.loop(0, per_block)
        def _(t):
            at = pl.multiple_of(t * TILE, TILE)
            body(pl.ds(pl.multiple_of(rows_at(r, c) + at, TILE), TILE), pl.ds(at, TILE))

    def strips(body):
        @pl.loop(0, own // STRIP)
        def _(t):
            body(pl.ds(pl.multiple_of(t * STRIP, STRIP), STRIP))

    base_copy = 14 + count - 1
    halves = [pl.ds(h * (width // 2), width // 2) for h in range(2)]
    span = 3 * channels // count

    def piece_rows(index):
        return pl.ds(pl.multiple_of(index * span, 16), span)

    piece_copies = [
        mp_copy(
            wmix.at[piece_rows(place), cols],
            gm.at[piece_rows(place), cols],
            across,
            base_copy + h,
        )
        for h, cols in enumerate(halves)
    ]
    outw_far = gm.at[pl.ds(3 * channels, channels)]
    outw_copy = mp_copy(outw, outw_far, across, base_copy + 11 + 3 * per_block)
    taps_copy = mp_copy(taps, taps2, across, base_copy + 2)
    cot_block = block_of(acts.at[1], 0, mine)
    cot_far = block_of(acts.at[1], 1, mine)
    cot_across = mp_copy(cot_block, cot_far, across, base_copy + 3)
    cot_core = mp_copy(cot_block, cot_block, partner, base_copy + 4)
    cot_pass = mp_copy(cot_far, cot_far, partner, base_copy + 5)
    n1_core = mp_copy(sa.at[mine], sa.at[mine], partner, base_copy + 6)
    n1_far = gm.at[pl.ds(pl.multiple_of(mine * own, own), own)]
    n1_across = mp_copy(sa.at[mine], n1_far, across, base_copy + 7)
    n1_pass = mp_copy(n1_far, n1_far, partner, base_copy + 8)

    def branch_sum(t):
        rows = pl.ds(pl.multiple_of(t * TILE, TILE), TILE)
        number = base_copy + 11 + 2 * per_block + t
        return mp_copy(xr.at[rows], ra.at[0, rows], partner, number)

    n2_block = block_of(acts.at[0], 0, mine)
    n2_core = mp_copy(n2_block, n2_block, partner, base_copy + 10)

    def n2_rows(r, t):
        return acts.at[0, pl.ds(pl.multiple_of(rows_at(r, mine) + t * TILE, TILE), TILE)]

    n2_across = [
        mp_copy(n2_rows(0, t), n2_rows(1, t), across, base_copy + 11 + t) for t in range(per_block)
    ]
    n2_pass = [
        mp_copy(n2_rows(1, t), n2_rows(1, t), partner, base_copy + 11 + per_block + t)
        for t in range(per_block)
    ]

    inw_load.wait()
    for copy in piece_copies:
        copy.start()
    taps[...] = jnp.zeros_like(taps)
    taps[0:3, :] = conv_ref[...].astype(F32)
    taps_copy.start()
    outw_load.wait()
    outw_copy.start()
    cot_load.wait()
    cot_across.start()
    tok_load.wait()

    own_length = lengths[me_mp // 2]

    def own_mask(rows):
        position = lax.broadcasted_iota(jnp.int32, (STRIP, 1), 0) + (core * own + rows.start)
        return (position < own_length).astype(F32)

    def first_norm(rows):
        x_rows = ra[1, rows].astype(F32)
        sa[mine, rows] = (own_mask(rows) * x_rows * rms_scale(x_rows) * gain1[...]).astype(BF16)

    strips(first_norm)
    n1_core.start()
    cot_core.start()

    far = count // 2

    def gather_copy(sub, h, index, number):
        piece = gm.at[piece_rows(lax.rem(index + 2 * count, count)), halves[sub]]
        return ring_copy(piece, piece, sub, h, number)

    for sub in range(2):
        piece_copies[sub].wait_recv()
        for h in range(2):
            gather_copy(sub, h, place, 0).start()

    def gather_hop(hop):
        for sub in range(2):
            for h in range(2):
                arrived = gather_copy(sub, h, place - signs[h] * hop, hop - 1)
                arrived.wait_recv()

                @pl.when(hop < (far if sub == h else far - 1))
                def _():
                    gather_copy(sub, h, place - signs[h] * hop, hop).start()

    def gather_last():
        for h in range(2):
            gather_copy(h, h, place - signs[h] * far, far - 1).wait_recv()
        for number in range(far):
            for sub in range(2):
                for h in range(2):
                    if number < far - 1 or sub == h:
                        gather_copy(sub, h, place, number).wait_send()

    seq_tiles = 2 * per_block

    def project(normed, weights):
        three = dot(normed, weights[0 : 3 * channels], 1, 1)
        return [three[:, k * channels : (k + 1) * channels] for k in range(3)]

    def convolve(mixed, tap_ref):
        mbuf[EDGE:, :] = mixed
        two_back, one_back = mbuf[EDGE - 2 : -2, :], mbuf[EDGE - 1 : -1, :]
        tap = [tap_ref[k : k + 1, :] for k in range(3)]
        conv = tap[0] * two_back + tap[1] * one_back + tap[2] * mixed
        return conv, (two_back, one_back, mixed)

    def carry(mixed):
        mbuf[0:EDGE, :] = mixed[TILE - EDGE :, :]

    def tile_rows(t):
        return pl.ds(pl.multiple_of(t * TILE, TILE), TILE)

    def mixer_tile(weights, tap_ref, at, t):
        normed = sa[t // per_block, tile_rows(lax.rem(t, per_block))]
        left, middle, right = project(normed, weights)
        mixed = left * right
        conv, _ = convolve(mixed, tap_ref)
        carry(mixed)
        aa[tile_rows(t), at * channels : (at + 1) * channels] = (middle * conv).astype(BF16)

    n1_core.wait_recv()
    for item in n1_stores:
        item.start()
    mbuf[0:EDGE, :] = jnp.zeros((EDGE, channels), F32)

    @pl.loop(0, seq_tiles)
    def _(t):
        mixer_tile(wmix, taps, 0, t)

        @pl.when(t + 1 < far)
        def _():
            gather_hop(t + 1)

    assert seq_tiles + 1 >= far
    gather_last()
    taps_copy.wait_recv()
    mbuf[0:EDGE, :] = jnp.zeros((EDGE, channels), F32)

    @pl.loop(0, seq_tiles)
    def _(t):
        mixer_tile(gm, taps2, 1, t)

    outw_copy.wait_recv()

    def branch(c, t):
        rows = pl.ds(pl.multiple_of(c * own + t * TILE, TILE), TILE)
        return dot(aa[rows, 0:channels], outw[...], 1, 0) + dot(
            aa[rows, channels : 2 * channels], outw_far[...], 1, 0
        )

    @pl.loop(0, per_block)
    def _(t):
        xr[pl.ds(pl.multiple_of(t * TILE, TILE), TILE), :] = branch(theirs, t).astype(BF16)
        branch_sum(t).start()

    @pl.loop(0, per_block)
    def _(t):
        f1[pl.ds(pl.multiple_of(t * TILE, TILE), TILE), :] = branch(mine, t)

    first_row = rows_at(0, mine)

    def own_rows(rows):
        return pl.ds(pl.multiple_of(first_row + rows.start, STRIP), STRIP)

    def second_norm(rows):
        hidden = ra[1, rows].astype(F32) + f1[rows] + ra[0, rows].astype(F32)
        f2[rows] = hidden
        acts[0, own_rows(rows)] = (hidden * rms_scale(hidden) * gain2[...]).astype(BF16)

    for t in range(per_block):
        branch_sum(t).wait()

        @pl.loop(0, TILE // STRIP)
        def _(i):
            second_norm(pl.ds(pl.multiple_of(t * TILE + i * STRIP, STRIP), STRIP))

        n2_across[t].start()
    n2_core.start()
    cot_across.wait_recv()
    cot_pass.start()

    def forward_tile(c, start):
        rows = pl.ds(pl.multiple_of(start, TILE), TILE)
        at = pl.multiple_of(c * chunk, chunk)
        both = pl.multiple_of(2 * c * chunk, chunk)
        pre = dot(acts[0, rows], wgu[pl.ds(both, 2 * chunk)], 1, 1)
        grad_activ = dot(acts[1, rows], wd[pl.ds(at, chunk)], 1, 1)
        gate_pre, up_pre = pre[:, :chunk], pre[:, chunk:]
        squash = 0.5 + 0.5 * jnp.tanh(0.5 * gate_pre)
        silu = gate_pre * squash
        aa[rows, pl.ds(at, chunk)] = (silu * up_pre).astype(BF16)
        slope = squash + silu - silu * squash
        agu[rows, pl.ds(both, chunk)] = (grad_activ * up_pre * slope).astype(BF16)
        agu[rows, pl.ds(both + chunk, chunk)] = (grad_activ * silu).astype(BF16)

    def weight_grad(c, part, rows):
        if part < 2:
            cols = pl.ds(pl.multiple_of((2 * c + part) * chunk, chunk), chunk)
            return dot(agu[rows, cols], acts[0, rows], 0, 0)
        return dot(aa[rows, pl.ds(pl.multiple_of(c * chunk, chunk), chunk)], acts[1, rows], 0, 0)

    def weight_grads(c, rows, add):
        def store(into, total):
            if add:
                total = gf[c, into, :].astype(F32) + total
            gf[c, into, :] = total.astype(BF16)

        @pl.loop(0, 2)
        def _(part):
            into = pl.ds(pl.multiple_of(part * chunk, chunk), chunk)
            cols = pl.ds(pl.multiple_of((2 * c + part) * chunk, chunk), chunk)
            store(into, dot(agu[rows, cols], acts[0, rows], 0, 0))

        cols = pl.ds(c * chunk, chunk)
        store(pl.ds(2 * chunk, chunk), dot(aa[rows, cols], acts[1, rows], 0, 0))

    def tile_list(tiles, before):
        def pick(index, at):
            value = jnp.int32(tiles[0][index])
            for i, tile in enumerate(tiles):
                value = jnp.where(at == i, jnp.int32(tile[index]), value)
            return value

        @pl.loop(0, len(tiles))
        def _(at):
            for i, wait in before.items():
                pl.when(at == i)(wait)
            c, r, other, t = (pick(index, at) for index in range(4))
            at_core = mine + other * (theirs - mine)
            forward_tile(c, rows_at(r, at_core) + t * TILE)

    def ready(*items):
        def wait():
            for item in items:
                item.wait()

        return wait

    def near_partner():
        n2_core.wait_recv()
        cot_core.wait_recv()

    def far_own(t):
        def wait():
            n2_across[t].wait_recv()
            n2_pass[t].start()

        return wait

    def far_partner(t):
        def wait():
            n2_pass[t].wait_recv()
            if t == 0:
                cot_pass.wait_recv()

        return wait

    def whole_block(c, r, other):
        return [(c, r, other, t) for t in range(per_block)]

    tile_list(
        whole_block(0, 0, 0) + whole_block(0, 0, 1),
        {0: ready(*weight_loads(0)), per_block: near_partner},
    )
    near, distant = pl.ds(0, 2 * own), pl.ds(2 * own, 2 * own)
    weight_grads(0, near, False)
    order, before = [], {}
    fillers = whole_block(1, 0, 0) + whole_block(1, 0, 1) + whole_block(2, 0, 0)
    fill = len(fillers) // (2 * per_block - 1)
    before[0] = ready(*weight_loads(1))
    for other, t in ((0, 0), (1, 0)) + tuple((o, t) for t in range(1, per_block) for o in (0, 1)):
        taken = fillers[:fill]
        fillers = fillers[fill:]
        for tile in taken:
            if tile[0] == 2 and not any(held[0] == 2 for held in order):
                before[len(order)] = ready(*weight_loads(2))
            order.append(tile)
        before[len(order)] = (far_partner if other else far_own)(t)
        order.append((0, 1, other, t))
    tile_list(order, before)
    n1_across.start()
    weight_grads(0, distant, True)
    sum_start(0)

    def far_tiles(*blocks):
        for block in blocks:
            tile_list(whole_block(*block), {})
            pump()

    def chunk_grads(c):
        weight_grads(c, pl.ds(0, group), False)
        pump()
        sum_start(c)
        pump()

    far_tiles((1, 1, 0), (1, 1, 1))
    chunk_grads(1)
    far_tiles((2, 0, 1), (2, 1, 0), (2, 1, 1))
    for copy in (
        piece_copies
        + n2_across
        + n2_pass
        + [taps_copy, outw_copy, cot_across, cot_core, cot_pass, n1_core, n1_across, n2_core]
    ):
        copy.wait_send()
    for item in n1_stores:
        item.wait()
    def gn2(rows):
        return dot(agu[rows, :], wgu[...], 1, 0)

    def to_send(r):
        def body(rows, local):
            sa[r, local] = gn2(rows).astype(BF16)

        return body

    def to_f1(rows, local):
        f1[local] = gn2(rows)

    core_copies = [mp_copy(sa.at[r], ra.at[r], partner, r) for r in range(2)]
    block_tiles(1, theirs, to_send(1))
    core_copies[1].start()
    pump()
    block_tiles(1, mine, to_f1)
    core_copies[1].wait_recv()

    def join(rows):
        ra[1, rows] = (ra[1, rows].astype(F32) + f1[rows]).astype(BF16)

    strips(join)
    across_copies = []
    for h, number in enumerate((2, base_copy + 12 + 3 * per_block)):
        rows = pl.ds(h * (own // 2), own // 2)
        across_copies.append(mp_copy(ra.at[1, rows], xr.at[rows], across, number))
        across_copies[h].start()
    pump()
    chunk_grads(2)
    pl.semaphore_signal(credit.at[2], inc=1, device_id=across, device_id_type=MESH)
    block_tiles(0, theirs, to_send(0))
    core_copies[0].start()
    pump()
    block_tiles(0, mine, to_f1)
    pump()
    n1_across.wait_recv()
    n1_pass.start()

    pump()
    n1_pass.wait()
    n1_load.start()
    n1_move.start()
    core_copies[0].wait_recv()
    smv[...] = jnp.zeros_like(smv)

    def hidden_grad(rows):
        grad = f1[rows] + ra[0, rows].astype(F32) + xr[rows].astype(F32)
        hidden = f2[rows]
        scale = rms_scale(hidden)
        smv[1:2, :] += jnp.sum(grad * hidden * scale, axis=0, keepdims=True)
        total = acts[1, own_rows(rows)].astype(F32) + rms_back(grad * gain2[...], hidden, scale)
        f1[rows] = total
        acts[1, own_rows(rows)] = total.astype(BF16)

    def block_ref(r, c, h):
        return acts.at[1, pl.ds(pl.multiple_of(rows_at(r, c) + h * (own // 2), STRIP), own // 2)]

    def branch_copy(source, target, device, number):
        return [
            mp_copy(block_ref(*source, h), block_ref(*target, h), device, number[h])
            for h in range(2)
        ]

    more = base_copy + 13 + 3 * per_block
    branch_across = branch_copy((0, mine), (1, mine), across, (3, more))
    branch_core = branch_copy((0, mine), (0, mine), partner, (4, more + 1))
    branch_pass = branch_copy((1, mine), (1, mine), partner, (5, more + 2))
    for h in range(2):
        if h == 1:
            pump()
        across_copies[h].wait_recv()

        @pl.loop(h * (own // 2 // STRIP), (h + 1) * (own // 2 // STRIP))
        def _(t):
            hidden_grad(pl.ds(pl.multiple_of(t * STRIP, STRIP), STRIP))

        if h == 1:
            for copy in core_copies + across_copies:
                copy.wait_send()
        if h == 0:
            pl.semaphore_wait(credit.at[2], 1)
        branch_across[h].start()
        branch_core[h].start()
    pump()

    def out_block(r, c, slot):
        def body(rows, local):
            to = pl.ds(pl.multiple_of(slot * own + local.start, TILE), TILE)
            agu[to, 0:width] = dot(aa[rows, :], wd[...], 1, 0).astype(BF16)

        block_tiles(r, c, body)

    for slot, (r, c) in enumerate(((1, theirs), (0, theirs), (1, mine), (0, mine))):
        out_block(r, c, slot)
        pump()

    for copy in branch_core:
        copy.wait_recv()

    out_copies = [
        mp_copy(agu.at[pl.ds((1 - r) * own, own), pl.ds(0, width)], ra.at[r], partner, 6 + r)
        for r in range(2)
    ]
    for r in (1, 0):
        out_copies[r].start()
    n1_load.wait()
    n1_move.wait()

    def mixer(r):
        def rows_of(t):
            return pl.ds(pl.multiple_of(2 * r * own + t * TILE, TILE), TILE)

        def finish(t):
            tap = [taps[k : k + 1, :] for k in range(3)]
            grad_mixed = (
                tap[2] * gbuf[0:TILE, :]
                + tap[1] * gbuf[1 : TILE + 1, :]
                + tap[0] * gbuf[2 : TILE + 2, :]
            )
            for k, kept in ((0, 1), (2, 0)):
                aa[rows_of(t), k * channels : (k + 1) * channels] = (
                    grad_mixed * pbuf[kept]
                ).astype(BF16)

        mbuf[0:EDGE, :] = jnp.zeros((EDGE, channels), F32)

        @pl.loop(0, seq_tiles)
        def _(t):
            rows = rows_of(t)
            left, middle, right = project(acts[0, rows], wmix)
            mixed = left * right
            conv, shifted = convolve(mixed, taps)
            aa[rows, 3 * channels : 4 * channels] = (middle * conv).astype(BF16)
            grad_mixer = dot(acts[1, rows], outw[...], 1, 1)
            aa[rows, channels : 2 * channels] = (grad_mixer * conv).astype(BF16)
            grad_conv = grad_mixer * middle
            for k, factor in enumerate(shifted):
                smv[2 + k : 3 + k, 0:channels] += jnp.sum(
                    grad_conv * factor, axis=0, keepdims=True
                )
            carry(mixed)

            @pl.when(t > 0)
            def _():
                gbuf[TILE:, :] = grad_conv[0:EDGE, :]
                finish(t - 1)

            gbuf[0:TILE, :] = grad_conv
            pbuf[0] = left
            pbuf[1] = right

        gbuf[TILE:, :] = jnp.zeros((EDGE, channels), F32)
        finish(seq_tiles - 1)

    mixer(0)
    pump()
    pump()

    branch_across[0].wait_recv()
    branch_pass[0].start()
    pump()
    branch_across[1].wait_recv()
    branch_pass[1].start()

    out_copies[1].wait_recv()

    def join_out(rows):
        kept = agu[pl.ds(pl.multiple_of(2 * own + rows.start, STRIP), STRIP), 0:width]
        ra[1, rows] = (ra[1, rows].astype(F32) + kept.astype(F32)).astype(BF16)

    strips(join_out)
    out_across = mp_copy(ra.at[1], xr, across, 8)
    out_across.start()
    pump()
    for copy in branch_pass:
        copy.wait_recv()
    mixer(1)
    pump()

    chunk_end(0)
    for device in (beside, along):
        pl.semaphore_signal(slots_free, inc=1, device_id=device, device_id_type=MESH)

    @pl.when(inside)
    def _():
        pl.semaphore_signal(slots_free, inc=1, device_id=middle, device_id_type=MESH)

    for copy in branch_across + branch_core + branch_pass:
        copy.wait_send()

    for k in range(4):
        used = acts[1] if k == 3 else acts[0]
        cols = slice(k * channels, (k + 1) * channels)
        gm[cols, :] = dot(aa[:, cols], used, 0, 0).astype(BF16)
        pump()
    tok_again.start()

    @pl.when(inside)
    def _():
        pl.semaphore_wait(slots_free, 3)

    @pl.when(jnp.logical_not(inside))
    def _():
        pl.semaphore_wait(slots_free, 2)

    sum_start(CHUNKS)

    def gn1(rows):
        return dot(aa[rows, 0 : 3 * channels], inw[...], 1, 0)

    def to_stage(r):
        def body(rows, local):
            to = pl.ds(pl.multiple_of(r * own + local.start, TILE), TILE)
            agu[to, width : 2 * width] = gn1(rows).astype(BF16)

        return body

    def to_f2(rows, local):
        f2[local] = gn1(rows)

    back_copies = [
        mp_copy(agu.at[pl.ds(r * own, own), pl.ds(width, width)], ra.at[r], partner, 9 + r)
        for r in range(2)
    ]
    for r in (1, 0):
        block_tiles(r, theirs, to_stage(r))
        pump()
    pump()

    out_copies[0].wait_recv()
    out_across.wait_recv()

    def finish_out(rows):
        kept = agu[pl.ds(pl.multiple_of(3 * own + rows.start, STRIP), STRIP), 0:width]
        total = f2[rows] + kept.astype(F32) + ra[0, rows].astype(F32) + xr[rows].astype(F32)
        sa[0, rows] = total.astype(BF16)

    strips(finish_out)
    out_store.start()
    for copy in out_copies + [out_across]:
        copy.wait_send()
    pl.semaphore_signal(credit.at[0], inc=1, device_id=partner, device_id_type=MESH)
    pl.semaphore_signal(credit.at[1], inc=1, device_id=across, device_id_type=MESH)

    pump()
    pl.semaphore_wait(credit.at[0], 1)
    pl.semaphore_wait(credit.at[1], 1)
    for r in (1, 0):
        back_copies[r].start()
    block_tiles(1, mine, to_f2)
    pump()
    pump()
    back_copies[1].wait_recv()

    def join_back(rows):
        ra[1, rows] = (ra[1, rows].astype(F32) + f2[rows]).astype(BF16)

    strips(join_back)
    back_across = mp_copy(ra.at[1], xr, across, 11)
    back_across.start()
    block_tiles(0, mine, to_f2)
    pump()
    pump()
    back_copies[0].wait_recv()
    back_across.wait_recv()

    def tokens_grad(rows):
        grad = f2[rows] + ra[0, rows].astype(F32) + xr[rows].astype(F32)
        grad = grad * own_mask(rows)
        x_rows = acts[0, rows].astype(F32)
        scale = rms_scale(x_rows)
        smv[0:1, :] += jnp.sum(grad * x_rows * scale, axis=0, keepdims=True)
        total = f1[rows] + rms_back(grad * gain1[...], x_rows, scale)
        sa[1, rows] = total.astype(BF16)

    tok_again.wait()
    strips(tokens_grad)
    tg_store.start()
    chunk_end(1)
    for copy in back_copies + [back_across]:
        copy.wait_send()

    small_core = mp_copy(smv, smb.at[0], partner, 12)
    small_core.start()
    pump()
    small_core.wait()
    smv[0:2, :] += smb[0, 0:2]
    small_across = mp_copy(smv, smb.at[1], across, 13)
    small_across.start()
    pump()
    small_across.wait()
    smv[0:2, :] += smb[1, 0:2]
    for hop, device in enumerate((beside, along, opposite)):
        swap = mp_copy(smv, smb.at[2 + hop], device, 14 + hop)
        swap.start()
        pump()
        swap.wait()
        smv[...] += smb[2 + hop]
    small_out[...] = smv[...]
    chunk_end(2)
    pump()
    assert next(sites, None) is None
    for number in range(CUT * CHUNKS, len(parts_list)):
        parts_list[number][2]()
    for item in mixer_stores:
        item.start()
    for item in grad_stores + mixer_stores:
        item.wait()
    out_store.wait()
    tg_store.wait()


def block_by_kernel(
    tokens,
    lengths,
    norm1_gain,
    in_weight,
    conv_weight,
    out_weight,
    norm2_gain,
    gate_weight,
    up_weight,
    down_weight,
    cotangent,
):
    count = lax.axis_size("dp")
    own, width = tokens.shape
    group = 4 * own
    channels = out_weight.shape[0]
    units = gate_weight.shape[0]
    chunk = units // CHUNKS
    part_rows, first = 3 * chunk // CUT, 5 * width // 8
    mp_copies = 14 + count - 1 + 16 + 3 * (own // TILE)
    anywhere = pl.BlockSpec(memory_space=pl.ANY)
    inside = pl.BlockSpec(memory_space=pltpu.VMEM)
    macs = group * width * (3 * 3 * units + 15 * channels)
    outs = pl.pallas_call(
        functools.partial(block_kernel, count),
        out_shape=(
            jax.ShapeDtypeStruct((own, width), BF16),
            jax.ShapeDtypeStruct((own, width), BF16),
            jax.ShapeDtypeStruct((units, width), BF16),
            jax.ShapeDtypeStruct((units, width), BF16),
            jax.ShapeDtypeStruct((units, width), BF16),
            jax.ShapeDtypeStruct((3 * channels, width), BF16),
            jax.ShapeDtypeStruct((channels, width), BF16),
            jax.ShapeDtypeStruct((8, width), F32),
            jax.ShapeDtypeStruct((2 * own, width), BF16),
        ),
        in_specs=[anywhere] * 7 + [inside] * 3 + [pl.BlockSpec(memory_space=pltpu.SMEM)],
        out_specs=(anywhere,) * 7 + (inside, anywhere),
        scratch_shapes=[
            pltpu.VMEM((2, group, width), BF16),
            pltpu.VMEM((2 * units, width), BF16),
            pltpu.VMEM((units, width), BF16),
            pltpu.VMEM((group, 2 * units), BF16),
            pltpu.VMEM((group, units), BF16),
            pltpu.VMEM((CHUNKS, 3 * chunk, width), BF16),
            pltpu.VMEM((CUT * CHUNKS, part_rows // 2, first), BF16),
            pltpu.VMEM((CUT * CHUNKS, 2, part_rows // 4, first), BF16),
            pltpu.VMEM((CUT * CHUNKS, 2, part_rows // 2, width - first), BF16),
            pltpu.VMEM((4 * channels, width), BF16),
            pltpu.VMEM((2, own, width), BF16),
            pltpu.VMEM((2, own, width), BF16),
            pltpu.VMEM((own, width), BF16),
            pltpu.VMEM((4 * channels, width), BF16),
            pltpu.VMEM((own, width), F32),
            pltpu.VMEM((own, width), F32),
            pltpu.VMEM((8, channels), F32),
            pltpu.VMEM((8, channels), F32),
            pltpu.VMEM((EDGE + TILE, channels), F32),
            pltpu.VMEM((TILE + EDGE, channels), F32),
            pltpu.VMEM((2, TILE, channels), F32),
            pltpu.VMEM((8, width), F32),
            pltpu.VMEM((5, 8, width), F32),
            pltpu.SemaphoreType.DMA((3 * CHUNKS + 10 + 3 * CHUNKS + 2,)),
            pltpu.SemaphoreType.DMA((2, 2, count // 2)),
            pltpu.SemaphoreType.DMA((2, 2, count // 2)),
            pltpu.SemaphoreType.DMA((CUT * CHUNKS + SLABS, 11)),
            pltpu.SemaphoreType.DMA((CUT * CHUNKS + SLABS, 11)),
            pltpu.SemaphoreType.REGULAR((CUT * CHUNKS + SLABS,)),
            pltpu.SemaphoreType.REGULAR((CUT * CHUNKS + SLABS,)),
            pltpu.SemaphoreType.REGULAR,
            pltpu.SemaphoreType.DMA((mp_copies,)),
            pltpu.SemaphoreType.DMA((mp_copies,)),
            pltpu.SemaphoreType.REGULAR((3,)),
        ],
        compiler_params=pltpu.CompilerParams(
            collective_id=0, has_side_effects=True, vmem_limit_bytes=VMEM_BYTES
        ),
        cost_estimate=pl.CostEstimate(
            flops=2 * macs, bytes_accessed=64 * 2**20, transcendentals=group * units
        ),
        name="block",
    )(
        tokens,
        cotangent,
        gate_weight,
        up_weight,
        down_weight,
        in_weight.reshape(3 * channels, width),
        out_weight,
        conv_weight,
        norm1_gain.reshape(1, width),
        norm2_gain.reshape(1, width),
        lengths,
    )
    held = 2 * own + 3 * units + 4 * channels
    finals = pl.pallas_call(
        widen_kernel,
        out_shape=(
            jax.ShapeDtypeStruct((own, width), BF16),
            jax.ShapeDtypeStruct((own, width), BF16),
            jax.ShapeDtypeStruct((units, width), F32),
            jax.ShapeDtypeStruct((units, width), F32),
            jax.ShapeDtypeStruct((units, width), F32),
            jax.ShapeDtypeStruct((3 * channels, width), F32),
            jax.ShapeDtypeStruct((channels, width), F32),
            jax.ShapeDtypeStruct((1, width), F32),
            jax.ShapeDtypeStruct((1, width), F32),
            jax.ShapeDtypeStruct((3, channels), F32),
        ),
        in_specs=[anywhere] * 7 + [inside],
        out_specs=(anywhere,) * 7 + (inside,) * 3,
        scratch_shapes=[
            pltpu.VMEM((held, width), BF16),
            pltpu.VMEM((held, width), F32),
            pltpu.SemaphoreType.DMA((2 * held // LANES,)),
        ],
        compiler_params=pltpu.CompilerParams(vmem_limit_bytes=WIDEN_BYTES),
        cost_estimate=pl.CostEstimate(flops=0, bytes_accessed=32 * 2**20, transcendentals=0),
        name="widen",
    )(*outs[:8])
    result, grad_tokens, gate_grad, up_grad, down_grad, in_grad, out_grad, one, two, taps = finals
    return (
        result,
        grad_tokens,
        one.reshape(width),
        in_grad.reshape(3, channels, width),
        taps,
        out_grad,
        two.reshape(width),
        gate_grad,
        up_grad,
        down_grad,
    )


def widen_kernel(*refs):
    sources, small = refs[:7], refs[7]
    targets, one, two, taps = refs[8:15], refs[15], refs[16], refs[17]
    narrow, wide, sem = refs[18:]
    reads, writes = [], []
    at = 0
    for i, (source, target) in enumerate(zip(sources, targets)):
        for row in range(0, source.shape[0], LANES):
            rows, held = pl.ds(row, LANES), pl.ds(at, LANES)
            number = 2 * (at // LANES)
            reads.append(pltpu.make_async_copy(source.at[rows], narrow.at[held], sem.at[number]))
            out = (narrow if i < 2 else wide).at[held]
            writes.append(pltpu.make_async_copy(out, target.at[rows], sem.at[number + 1]))
            at += LANES
    passed = 2 * sources[0].shape[0] // LANES
    for copy in reads:
        copy.start()
    one[...] = small[0:1, :]
    two[...] = small[1:2, :]
    taps[...] = small[2:5, : taps.shape[1]]
    for i, (read, write) in enumerate(zip(reads, writes)):
        read.wait()
        if i >= passed:
            rows = slice(i * LANES, (i + 1) * LANES)
            wide[rows, :] = narrow[rows, :].astype(F32)
        write.start()
    for copy in writes:
        copy.wait()


VMEM_BYTES = 62 * 2**20
WIDEN_BYTES = 62 * 2**20


def on_device(
    tokens,
    lengths,
    norm1_gain,
    in_weight,
    conv_weight,
    out_weight,
    norm2_gain,
    gate_weight,
    up_weight,
    down_weight,
    cotangent,
):
    assert 2 * tokens.shape[0] == SEQ_LEN
    fits = lax.axis_size("mp") == 4 and lax.axis_size("dp") == 8
    block = block_by_kernel if fits else block_by_ops
    return block(
        tokens,
        lengths,
        norm1_gain,
        in_weight,
        conv_weight,
        out_weight,
        norm2_gain,
        gate_weight,
        up_weight,
        down_weight,
        cotangent,
    )


def solution(mesh):
    rows = P(("dp", "mp"), None)
    hidden_rows = P("mp", None)
    placed = (
        rows,
        P("dp"),
        P(),
        P(None, "mp", None),
        P(None, "mp"),
        hidden_rows,
        P(),
        hidden_rows,
        hidden_rows,
        hidden_rows,
        rows,
    )
    return jax.shard_map(
        on_device,
        mesh=mesh,
        in_specs=placed,
        out_specs=(
            rows,
            rows,
            P(),
            P(None, "mp", None),
            P(None, "mp"),
            hidden_rows,
            P(),
            hidden_rows,
            hidden_rows,
            hidden_rows,
        ),
        check_vma=False,
    )
```

```python
import functools

import jax
import jax.numpy as jnp
from jax import lax
from jax.experimental import pallas as pl
from jax.experimental.pallas import tpu as pltpu
from jax.sharding import PartitionSpec as P

SEQ_LEN = 1024
NORM_EPS = 1e-05
F32 = jnp.float32
BF16 = jnp.bfloat16
MESH = pl.DeviceIdType.MESH
LANES = 128


def rms_scale(row_data):
    return lax.rsqrt(jnp.mean(row_data * row_data, axis=-1, keepdims=True) + NORM_EPS)


def rms_back(grad_scaled, row_data, scale_rows):
    inner_mean = jnp.mean(grad_scaled * row_data, axis=-1, keepdims=True)
    return scale_rows * grad_scaled - row_data * (scale_rows * scale_rows * scale_rows) * inner_mean


def dot(left, right, left_dim, right_dim):
    return lax.dot_general(
        left, right, (((left_dim,), (right_dim,)), ((), ())), preferred_element_type=F32
    )


def to_partner(values):
    count = lax.axis_size("mp")
    return lax.ppermute(values, "mp", [(i, i ^ 1) for i in range(count)])


def to_chip(values, ahead):
    count = lax.axis_size("mp")
    return lax.ppermute(values, "mp", [(i, (i + 2 * ahead) % count) for i in range(count)])


def gather_rows(own):
    chips = lax.axis_size("mp") // 2
    first = lax.axis_index("mp") % 2 == 0
    mine = [own] + [to_chip(own, chips - r) for r in range(1, chips)]
    blocks = []
    for block in mine:
        other = to_partner(block)
        blocks += [jnp.where(first, block, other), jnp.where(first, other, block)]
    return jnp.concatenate(blocks, axis=0)


def scatter_sum(partial, own_rows):
    chips = lax.axis_size("mp") // 2
    first = lax.axis_index("mp") % 2 == 0
    blocks = partial.reshape(chips, 2, own_rows, partial.shape[-1])
    sums = []
    for r in range(chips):
        theirs = to_partner(jnp.where(first, blocks[r, 1], blocks[r, 0]))
        mine = jnp.where(first, blocks[r, 0], blocks[r, 1])
        sums.append(mine.astype(F32) + theirs.astype(F32))
    total = sums[0]
    for r in range(1, chips):
        total = total + to_chip(sums[r].astype(BF16), r).astype(F32)
    return total


def ring_place(device, count):
    z, y = device // 2, device % 2
    return y * (count - 1 - z) + (1 - y) * z


def ring_device(place, count):
    back = place // (count // 2)
    return (1 - back) * 2 * place + back * (2 * (count - 1 - place) + 1)


def ring_sum(pieces):
    count = lax.axis_size("dp")
    order = [ring_device(i, count) for i in range(count)]
    place = ring_place(lax.axis_index("dp"), count)
    right = [(order[i], order[(i + 1) % count]) for i in range(count)]
    left = [(b, a) for a, b in right]

    def take(source, half, index):
        return lax.dynamic_index_in_dim(source, half * count + index, 0, keepdims=False)

    total = jnp.zeros(pieces.shape, BF16)
    moving = [take(pieces, 0, place), take(pieces, 1, place)]
    for step in range(1, count):
        moving = [lax.ppermute(moving[0], "dp", right), lax.ppermute(moving[1], "dp", left)]
        at = [(place - step + count) % count, (place + step) % count]
        moving = [
            (moving[h].astype(F32) + take(pieces, h, at[h]).astype(F32)).astype(BF16)
            for h in range(2)
        ]
    at = [(place + 1) % count, (place - 1 + count) % count]
    for h in range(2):
        total = lax.dynamic_update_index_in_dim(total, moving[h], h * count + at[h], 0)
    for step in range(1, count):
        moving = [lax.ppermute(moving[0], "dp", right), lax.ppermute(moving[1], "dp", left)]
        at = [(place + 1 - step + count) % count, (place - 1 + step) % count]
        for h in range(2):
            total = lax.dynamic_update_index_in_dim(total, moving[h], h * count + at[h], 0)
    return total


def sum_weights(parts):
    count = 2 * lax.axis_size("dp")
    stacked = jnp.concatenate(
        [part.astype(BF16).reshape(count, part.shape[0] // count, part.shape[1]) for part in parts],
        axis=1,
    )
    total = ring_sum(stacked)
    results = []
    at = 0
    for part in parts:
        rows = part.shape[0] // count
        results.append(total[:, at : at + rows].reshape(part.shape).astype(F32))
        at += rows
    return results


def butterfly(values, axis):
    count = lax.axis_size(axis)
    step = 1
    while step < count:
        values = values + lax.ppermute(values, axis, [(i, i ^ step) for i in range(count)])
        step *= 2
    return values


def block_by_ops(
    tokens,
    lengths,
    norm1_gain,
    in_weight,
    conv_weight,
    out_weight,
    norm2_gain,
    gate_weight,
    up_weight,
    down_weight,
    cotangent,
):
    own_rows, width = tokens.shape
    chips = lax.axis_size("mp") // 2
    chip = lax.axis_index("mp") // 2
    core = lax.axis_index("mp") % 2
    positions = core * own_rows + jnp.arange(own_rows, dtype=jnp.int32)
    seq_slots = jnp.arange(lengths.shape[0], dtype=jnp.int32)
    own_length = jnp.sum(jnp.where(seq_slots == chip, lengths, 0))
    own_mask = (positions < own_length).astype(F32)[:, None]
    channels = in_weight.shape[1]
    group_rows = 2 * chips * own_rows
    x_rows = tokens.astype(F32)
    scale_one = rms_scale(x_rows)
    normed_one = (own_mask * x_rows * scale_one * norm1_gain).astype(BF16)
    normed_one_all = gather_rows(normed_one)
    proj, shifted, conv, mixer_out = mixer_forward(normed_one_all, in_weight, conv_weight, chips)
    branch = scatter_sum(dot(mixer_out, out_weight, 1, 0).astype(BF16), own_rows)
    hidden = x_rows + branch
    scale_two = rms_scale(hidden)
    normed_two = (hidden * scale_two * norm2_gain).astype(BF16)
    normed_two_all = gather_rows(normed_two)
    cot_all = gather_rows(cotangent)
    gate_pre = dot(normed_two_all, gate_weight, 1, 1)
    up_pre = dot(normed_two_all, up_weight, 1, 1)
    squash = jax.nn.sigmoid(gate_pre)
    activ = (gate_pre * squash * up_pre).astype(BF16)
    grad_activ = dot(cot_all, down_weight, 1, 1)
    grad_gate = (grad_activ * up_pre * squash * (1.0 + gate_pre * (1.0 - squash))).astype(BF16)
    grad_up = (grad_activ * gate_pre * squash).astype(BF16)
    down_grad = dot(activ, cot_all, 0, 0)
    gate_grad = dot(grad_gate, normed_two_all, 0, 0)
    up_grad = dot(grad_up, normed_two_all, 0, 0)
    down_grad, gate_grad, up_grad = sum_weights([down_grad, gate_grad, up_grad])

    grad_normed_two = scatter_sum(
        (dot(grad_gate, gate_weight, 1, 0) + dot(grad_up, up_weight, 1, 0)).astype(BF16), own_rows
    )
    gain_two = jnp.sum(grad_normed_two * hidden * scale_two, axis=0)
    grad_hidden = cotangent.astype(F32) + rms_back(grad_normed_two * norm2_gain, hidden, scale_two)
    branch_all = gather_rows(grad_hidden.astype(BF16))
    taps = conv_weight.astype(F32)
    out_grad = dot(mixer_out, branch_all, 0, 0)
    grad_mixer = dot(branch_all, out_weight, 1, 1).reshape(chips, 2 * own_rows, channels)
    grad_conv = grad_mixer * proj[1]
    conv_grad = jnp.stack([jnp.sum(grad_conv * shifted[k], axis=(0, 1)) for k in range(3)])
    grad_pad = jnp.pad(grad_conv, ((0, 0), (0, 2), (0, 0)))
    grad_mixed = (
        taps[2] * grad_conv
        + taps[1] * grad_pad[:, 1 : 1 + 2 * own_rows]
        + taps[0] * grad_pad[:, 2 : 2 + 2 * own_rows]
    )
    grad_proj = [
        piece.astype(BF16).reshape(group_rows, channels)
        for piece in (grad_mixed * proj[2], grad_mixer * conv, grad_mixed * proj[0])
    ]
    in_grad = [dot(piece, normed_one_all, 0, 0) for piece in grad_proj]
    in_grad_0, in_grad_1, in_grad_2, out_grad = sum_weights(in_grad + [out_grad])
    grad_normed_one = scatter_sum(
        sum(dot(grad_proj[k], in_weight[k], 1, 0) for k in range(3)).astype(BF16), own_rows
    )
    masked_grad = own_mask * grad_normed_one
    gain_one = jnp.sum(masked_grad * x_rows * scale_one, axis=0)
    grad_tokens = grad_hidden + rms_back(masked_grad * norm1_gain, x_rows, scale_one)
    gains = butterfly(jnp.concatenate([gain_one, gain_two]), "mp")
    small = butterfly(jnp.concatenate([gains, conv_grad.reshape(-1)]), "dp")
    result = hidden + scatter_sum(dot(activ, down_weight, 1, 0).astype(BF16), own_rows)
    return (
        result.astype(BF16),
        grad_tokens.astype(BF16),
        small[:width],
        jnp.stack([in_grad_0, in_grad_1, in_grad_2]),
        small[2 * width :].reshape(3, channels),
        out_grad,
        small[width : 2 * width],
        gate_grad,
        up_grad,
        down_grad,
    )


def mixer_forward(normed_one_all, in_weight, conv_weight, chips):
    rows = normed_one_all.shape[0] // chips
    channels = in_weight.shape[1]
    proj = [dot(normed_one_all, in_weight[k], 1, 1).reshape(chips, rows, channels) for k in range(3)]
    taps = conv_weight.astype(F32)
    mixed_pad = jnp.pad(proj[0] * proj[2], ((0, 0), (2, 0), (0, 0)))
    shifted = [mixed_pad[:, k : k + rows] for k in range(3)]
    conv = taps[0] * shifted[0] + taps[1] * shifted[1] + taps[2] * shifted[2]
    mixer_out = (proj[1] * conv).astype(BF16).reshape(chips * rows, channels)
    return proj, shifted, conv, mixer_out


CHUNKS = 3
TILE = 256
KINDS = (
    ("A1", "PF1", "PF2", "PF3", "PG1", "PG2", "PG3")
    + ("QF1", "QF2", "QF3", "QSW", "QG1", "QG2", "QG3")
)
AT_END = (
    (),
    (),
    (0,),
    (),
    (),
    (),
    (100,),
    (9, 200),
    (109, 300, 3),
    (10, 209, 110, 309),
    (),
    (),
    (103, 210),
    (),
    (),
    (203,),
    (),
    (),
    (303,),
    (400, 500, 409, 13),
    (310,),
    (),
    (),
    (509, 106, 410),
    (6, 510, 206, 113),
    (),
    (),
    (),
    (),
    (),
    (600,),
    (403, 213),
    (),
    (),
    (503, 700),
    (900, 609, 800, 709, 809, 909, 513, 306, 413),
    (610, 710, 810, 603, 910, 313, 703, 506, 803),
    (903, 406),
    (606,),
    (),
    (713,),
    (613, 706, 806, 906),
    (913, 813),
)
INSIDE = (
    (),
    (7,),
    (107,),
    (),
    (8, 0, 1),
    (108, 207),
    (2, 307, 100, 200, 208, 101),
    (308, 201, 300),
    (301, 102, 202, 4),
    (),
    (5, 11),
    (111, 302),
    (407,),
    (12,),
    (507, 112),
    (400, 104, 408),
    (),
    (),
    (508, 211),
    (204, 105),
    (304,),
    (212, 401),
    (205,),
    (500, 501, 305, 311, 402),
    (502, 411),
    (),
    (312, 511),
    (412,),
    (),
    (807, 607),
    (707, 512),
    (),
    (),
    (907, 608, 404, 600, 808, 708, 700),
    (601,),
    (908, 504),
    (
        900, 701, 405, 800, 901, 602, 801, 505, 702, 611, 802, 711, 902, 811, 612, 604, 812,
        911, 605, 704, 712,
    ),
    (804, 912, 904, 705),
    (805, 905),
    (),
    (),
    (),
    (),
)
CUT = 2
SLABS = 4
STRIP = 128
EDGE = 8


def block_kernel(
    count,
    tok_hbm,
    cot_hbm,
    gate_hbm,
    up_hbm,
    down_hbm,
    inw_hbm,
    outw_hbm,
    conv_ref,
    gain1,
    gain2,
    lengths,
    out_hbm,
    tg_hbm,
    gate_out,
    up_out,
    down_out,
    in_out,
    mix_out,
    small_out,
    n1_hbm,
    acts,
    wgu,
    wd,
    agu,
    aa,
    gf,
    land_a,
    land_p,
    land_q,
    gm,
    sa,
    ra,
    xr,
    wmix,
    f1,
    f2,
    taps,
    taps2,
    mbuf,
    gbuf,
    pbuf,
    smv,
    smb,
    ld_sem,
    ring_send,
    ring_recv,
    sum_send,
    sum_recv,
    half_free,
    rows_free,
    slots_free,
    mp_send,
    mp_recv,
    credit,
):
    own, width = out_hbm.shape
    group = 4 * own
    hidden_units = wd.shape[0]
    chunk = hidden_units // CHUNKS
    channels = outw_hbm.shape[0]
    per_block = own // TILE

    me_dp, me_mp = lax.axis_index("dp"), lax.axis_index("mp")
    core = me_mp % 2
    partner = (me_dp, me_mp + 1 - 2 * core)
    across = (me_dp, (me_mp + 2) % 4)
    place = ring_place(me_dp, count)
    nexts = [
        (ring_device((place + step) % count, count), me_mp) for step in (1, count - 1)
    ]
    signs = (1, -1)
    z, y = me_dp // 2, me_dp % 2
    side = z // 2
    inside = ((z + 1) // 2) % 2 == 1
    beside = (2 * z + 1 - y, me_mp)
    along = (2 * (z + 1 - 2 * (z % 2)) + y, me_mp)
    middle = (2 * (3 - z) + y, me_mp)
    opposite = (2 * ((z + 2) % 4) + y, me_mp)

    def rows_at(r, c):
        return pl.multiple_of((2 * r + c) * own, own)

    mine, theirs = core, 1 - core

    def load(src, dst, index):
        return pltpu.make_async_copy(src, dst, ld_sem.at[index])

    def weight_loads(c):
        at = pl.multiple_of(c * chunk, chunk)
        to = pl.multiple_of(2 * c * chunk, chunk)
        rows = pl.ds(at, chunk)
        return [
            load(gate_hbm.at[rows], wgu.at[pl.ds(to, chunk)], 3 * c),
            load(up_hbm.at[rows], wgu.at[pl.ds(to + chunk, chunk)], 3 * c + 1),
            load(down_hbm.at[rows], wd.at[rows], 3 * c + 2),
        ]

    def block_of(ref, r, c):
        return ref.at[pl.ds(rows_at(r, c), own)]

    inw = wmix.at[pl.ds(0, 3 * channels)]
    outw = wmix.at[pl.ds(3 * channels, channels)]
    late = 3 * CHUNKS
    inw_load = load(inw_hbm, inw, late)
    outw_load = load(outw_hbm, outw, late + 1)
    tok_load = load(tok_hbm, ra.at[1], late + 2)
    tok_again = load(tok_hbm, acts.at[0, pl.ds(0, own)], late + 2)
    cot_load = load(cot_hbm, block_of(acts.at[1], 0, mine), late + 3)
    n1_load = load(n1_hbm, acts.at[0, pl.ds(0, 2 * own)], late + 4)
    n1_move = load(gm.at[pl.ds(0, 2 * own)], acts.at[0, pl.ds(2 * own, 2 * own)], late + 9)
    out_store = load(sa.at[0], out_hbm, late + 5)
    tg_store = load(sa.at[1], tg_hbm, late + 6)
    n1_stores = [
        load(sa.at[c], n1_hbm.at[pl.ds(c * own, own)], late + 7 + c) for c in range(2)
    ]
    late += 10
    grad_stores = [
        load(
            gf.at[c, pl.ds(k * chunk, chunk)],
            ref.at[pl.ds(c * chunk, chunk)],
            late + CHUNKS * k + c,
        )
        for k, ref in enumerate((gate_out, up_out, down_out))
        for c in range(CHUNKS)
    ]
    late += 3 * CHUNKS
    slab_rows = 4 * channels // SLABS
    mixer_stores = []
    for k in range(SLABS):
        target = mix_out if k == SLABS - 1 else in_out.at[pl.ds(k * slab_rows, slab_rows)]
        mixer_stores.append(load(gm.at[pl.ds(k * slab_rows, slab_rows)], target, late + k))
    assert slab_rows == channels

    for item in (inw_load, outw_load, cot_load, tok_load):
        item.start()
    for c in range(CHUNKS):
        for item in weight_loads(c):
            item.start()

    barrier = pltpu.get_barrier_semaphore()
    for device in (partner, across, beside, along, opposite):
        pl.semaphore_signal(barrier, inc=1, device_id=device, device_id_type=MESH)

    @pl.when(inside)
    def _():
        pl.semaphore_signal(barrier, inc=1, device_id=middle, device_id_type=MESH)
        pl.semaphore_wait(barrier, 6)

    @pl.when(jnp.logical_not(inside))
    def _():
        pl.semaphore_wait(barrier, 5)

    def ring_copy(src, dst, lane, h, number):
        return pltpu.make_async_remote_copy(
            src_ref=src,
            dst_ref=dst,
            send_sem=ring_send.at[lane, h, number],
            recv_sem=ring_recv.at[lane, h, number],
            device_id=nexts[h],
            device_id_type=MESH,
        )

    first = 5 * width // 8

    def make_part(bucket, start, rows, landing, number):
        quarter, two = rows // 4, rows // 2

        def own_half(h):
            at = pl.multiple_of(start + h * two, 16)
            return bucket.at[pl.ds(at, two), pl.ds(0, first)]

        def part_p(f):
            at = pl.multiple_of(start + y * two + f * quarter, 16)
            return bucket.at[pl.ds(at, quarter), pl.ds(0, first)]

        def part_q(f):
            at = pl.multiple_of(start + f * two, 16)
            return bucket.at[pl.ds(at, two), pl.ds(first, width - first)]

        def send(index, src, dst, device):
            return pltpu.make_async_remote_copy(
                src_ref=src,
                dst_ref=dst,
                send_sem=sum_send.at[number, index],
                recv_sem=sum_recv.at[number, index],
                device_id=device,
                device_id_type=MESH,
            )

        def arrived(index, ref):
            send(index, ref, ref, beside).wait_recv()

        def sent(index, ref):
            send(index, ref, ref, beside).wait_send()

        def add(target, ref):
            target[...] = target[...] + ref[...]

        land_a, land_p, land_q = landing
        ours, other = side, 1 - side
        a1, p1, p2, q1, q2, pg1, pg2, qg1, qg2, ya, yb = range(11)

        def half_sum(f):
            return land_a.at[pl.ds(pl.multiple_of(f * quarter, 16), quarter)]

        def begin():
            send(a1, own_half(1 - y), land_a, beside).start()

            @pl.when(jnp.logical_not(inside))
            def _():
                send(q1, part_q(ours), land_q[0], along).start()

        told = set()

        def hand_over(index, f, at_end):
            if at_end not in told:
                told.add(at_end)
                pl.semaphore_wait(half_free.at[number], 1)
            send(index, part_p(f), part_p(f), beside).start()

        def sum_rows(kind, at_end):
            if kind == "A1":
                arrived(a1, land_a)
                add(land_a, own_half(y))
                if at_end:
                    send(p1, half_sum(ours), land_p[0], along).start()
                sent(a1, land_a)
                pl.semaphore_signal(
                    half_free.at[number], inc=1, device_id=beside, device_id_type=MESH
                )
            elif kind == "PF1":
                arrived(p1, land_p[0])
                add(land_p[0], half_sum(ours))
                send(p2, land_p[0], land_p[1], middle).start()
            elif kind == "PF2":
                arrived(p2, land_p[1])
                add(land_p[1], half_sum(other))
                send(p1, land_p[1], land_p[0], along).start()
            elif kind == "PF3":
                arrived(p1, land_p[0])
                part_p(other)[...] = land_p[0][...] + half_sum(other)[...]
                send(pg1, part_p(other), part_p(other), along).start()
                hand_over(ya, other, at_end)
            elif kind == "PG1":
                arrived(pg1, part_p(other))
                send(pg2, part_p(other), part_p(other), middle).start()
                hand_over(ya, other, at_end)
            elif kind == "PG2":
                arrived(pg2, part_p(ours))
                send(pg1, part_p(ours), part_p(ours), along).start()
                hand_over(yb, ours, at_end)
            elif kind == "PG3":
                arrived(pg1, part_p(ours))
                hand_over(yb, ours, at_end)
            elif kind == "QF1":
                arrived(q1, land_q[0])
                add(land_q[0], part_q(ours))
                send(q2, land_q[0], land_q[1], middle).start()
            elif kind == "QF2":
                arrived(q2, land_q[1])
                add(land_q[1], part_q(other))
                send(q1, land_q[1], land_q[0], along).start()
            elif kind == "QF3":
                arrived(q1, land_q[0])
                add(land_q[0], part_q(other))
                send(q2, land_q[0], land_q[1], beside).start()
                sent(q1, land_q[0])
                pl.semaphore_signal(
                    rows_free.at[number], inc=1, device_id=along, device_id_type=MESH
                )
            elif kind == "QSW":
                arrived(q2, land_q[1])
                part_q(other)[...] = land_q[0][...] + land_q[1][...]
                send(qg1, part_q(other), part_q(other), along).start()
            elif kind == "QG1":
                arrived(qg1, part_q(other))
                send(qg2, part_q(other), part_q(other), middle).start()
            elif kind == "QG2":
                arrived(qg2, part_q(ours))
                pl.semaphore_wait(rows_free.at[number], 1)
                send(qg1, part_q(ours), part_q(ours), along).start()
            elif kind == "QG3":
                arrived(qg1, part_q(ours))

        def end():
            for index, f in ((ya, other), (yb, ours)):
                at = pl.multiple_of(start + (1 - y) * two + f * quarter, 16)
                arrived(index, bucket.at[pl.ds(at, quarter), pl.ds(0, first)])
            for index in (p1, pg1, ya, yb):
                sent(index, part_p(0))
            for index in (q2, qg1):
                sent(index, part_q(0))

            @pl.when(inside)
            def _():
                for index in (p2, pg2):
                    sent(index, part_p(0))
                for index in (q1, qg2):
                    sent(index, part_q(0))

        return begin, sum_rows, end

    part_rows = 3 * chunk // CUT
    parts_list = []
    for c in range(CHUNKS):
        for k in range(CUT):
            slot = CUT * c + k
            landing = (
                land_a.at[slot],
                [land_p.at[slot, 0], land_p.at[slot, 1]],
                [land_q.at[slot, 0], land_q.at[slot, 1]],
            )
            parts_list.append(make_part(gf.at[c], k * part_rows, part_rows, landing, slot))
    for k in range(SLABS):
        slot, upper = k // 2, k % 2
        two, quarter = slab_rows // 2, slab_rows // 4
        landing = (
            land_a.at[slot, pl.ds(upper * two, two)],
            [land_p.at[slot, i, pl.ds(upper * quarter, quarter)] for i in range(2)],
            [land_q.at[slot, i, pl.ds(upper * two, two)] for i in range(2)],
        )
        parts_list.append(
            make_part(gm, k * slab_rows, slab_rows, landing, CUT * CHUNKS + k)
        )

    def sum_start(c):
        chosen = range(CUT * c, CUT * c + CUT) if c < CHUNKS else range(CUT * c, len(parts_list))
        for number in chosen:
            parts_list[number][0]()

    def chunk_end(c):
        for number in range(CUT * c, CUT * c + CUT):
            parts_list[number][2]()
        for item in grad_stores[c::CHUNKS]:
            item.start()

    sites = iter(zip(AT_END, INSIDE))

    def pump():
        at_end, within = next(sites)

        @pl.when(jnp.logical_not(inside))
        def _():
            for event in at_end:
                parts_list[event // 100][1](KINDS[event % 100], True)

        @pl.when(inside)
        def _():
            for event in within:
                parts_list[event // 100][1](KINDS[event % 100], False)

    def mp_copy(src, dst, device, number):
        return pltpu.make_async_remote_copy(
            src_ref=src,
            dst_ref=dst,
            send_sem=mp_send.at[number],
            recv_sem=mp_recv.at[number],
            device_id=device,
            device_id_type=MESH,
        )

    def block_tiles(r, c, body):
        @pl.loop(0, per_block)
        def _(t):
            at = pl.multiple_of(t * TILE, TILE)
            body(pl.ds(pl.multiple_of(rows_at(r, c) + at, TILE), TILE), pl.ds(at, TILE))

    def strips(body):
        @pl.loop(0, own // STRIP)
        def _(t):
            body(pl.ds(pl.multiple_of(t * STRIP, STRIP), STRIP))

    base_copy = 14 + count - 1
    halves = [pl.ds(h * (width // 2), width // 2) for h in range(2)]
    span = 3 * channels // count

    def piece_rows(index):
        return pl.ds(pl.multiple_of(index * span, 16), span)

    piece_copies = [
        mp_copy(
            wmix.at[piece_rows(place), cols],
            gm.at[piece_rows(place), cols],
            across,
            base_copy + h,
        )
        for h, cols in enumerate(halves)
    ]
    outw_far = gm.at[pl.ds(3 * channels, channels)]
    outw_copy = mp_copy(outw, outw_far, across, base_copy + 11 + 3 * per_block)
    taps_copy = mp_copy(taps, taps2, across, base_copy + 2)
    cot_block = block_of(acts.at[1], 0, mine)
    cot_far = block_of(acts.at[1], 1, mine)
    cot_across = mp_copy(cot_block, cot_far, across, base_copy + 3)
    cot_core = mp_copy(cot_block, cot_block, partner, base_copy + 4)
    cot_pass = mp_copy(cot_far, cot_far, partner, base_copy + 5)
    n1_core = mp_copy(sa.at[mine], sa.at[mine], partner, base_copy + 6)
    n1_far = gm.at[pl.ds(pl.multiple_of(mine * own, own), own)]
    n1_across = mp_copy(sa.at[mine], n1_far, across, base_copy + 7)
    n1_pass = mp_copy(n1_far, n1_far, partner, base_copy + 8)

    def branch_sum(t):
        rows = pl.ds(pl.multiple_of(t * TILE, TILE), TILE)
        number = base_copy + 11 + 2 * per_block + t
        return mp_copy(xr.at[rows], ra.at[0, rows], partner, number)

    n2_block = block_of(acts.at[0], 0, mine)
    n2_core = mp_copy(n2_block, n2_block, partner, base_copy + 10)

    def n2_rows(r, t):
        return acts.at[0, pl.ds(pl.multiple_of(rows_at(r, mine) + t * TILE, TILE), TILE)]

    n2_across = [
        mp_copy(n2_rows(0, t), n2_rows(1, t), across, base_copy + 11 + t) for t in range(per_block)
    ]
    n2_pass = [
        mp_copy(n2_rows(1, t), n2_rows(1, t), partner, base_copy + 11 + per_block + t)
        for t in range(per_block)
    ]

    inw_load.wait()
    for copy in piece_copies:
        copy.start()
    taps[...] = jnp.zeros_like(taps)
    taps[0:3, :] = conv_ref[...].astype(F32)
    taps_copy.start()
    outw_load.wait()
    outw_copy.start()
    cot_load.wait()
    cot_across.start()
    tok_load.wait()

    own_length = lengths[me_mp // 2]

    def own_mask(rows):
        position = lax.broadcasted_iota(jnp.int32, (STRIP, 1), 0) + (core * own + rows.start)
        return (position < own_length).astype(F32)

    def first_norm(rows):
        x_rows = ra[1, rows].astype(F32)
        sa[mine, rows] = (own_mask(rows) * x_rows * rms_scale(x_rows) * gain1[...]).astype(BF16)

    strips(first_norm)
    n1_core.start()
    cot_core.start()

    far = count // 2

    def gather_copy(sub, h, index, number):
        piece = gm.at[piece_rows(lax.rem(index + 2 * count, count)), halves[sub]]
        return ring_copy(piece, piece, sub, h, number)

    for sub in range(2):
        piece_copies[sub].wait_recv()
        for h in range(2):
            gather_copy(sub, h, place, 0).start()

    def gather_hop(hop):
        for sub in range(2):
            for h in range(2):
                arrived = gather_copy(sub, h, place - signs[h] * hop, hop - 1)
                arrived.wait_recv()

                @pl.when(hop < (far if sub == h else far - 1))
                def _():
                    gather_copy(sub, h, place - signs[h] * hop, hop).start()

    def gather_last():
        for h in range(2):
            gather_copy(h, h, place - signs[h] * far, far - 1).wait_recv()
        for number in range(far):
            for sub in range(2):
                for h in range(2):
                    if number < far - 1 or sub == h:
                        gather_copy(sub, h, place, number).wait_send()

    seq_tiles = 2 * per_block

    def project(normed, weights):
        three = dot(normed, weights[0 : 3 * channels], 1, 1)
        return [three[:, k * channels : (k + 1) * channels] for k in range(3)]

    def convolve(mixed, tap_ref):
        mbuf[EDGE:, :] = mixed
        two_back, one_back = mbuf[EDGE - 2 : -2, :], mbuf[EDGE - 1 : -1, :]
        tap = [tap_ref[k : k + 1, :] for k in range(3)]
        conv = tap[0] * two_back + tap[1] * one_back + tap[2] * mixed
        return conv, (two_back, one_back, mixed)

    def carry(mixed):
        mbuf[0:EDGE, :] = mixed[TILE - EDGE :, :]

    def tile_rows(t):
        return pl.ds(pl.multiple_of(t * TILE, TILE), TILE)

    def mixer_tile(weights, tap_ref, at, t):
        normed = sa[t // per_block, tile_rows(lax.rem(t, per_block))]
        left, middle, right = project(normed, weights)
        mixed = left * right
        conv, _ = convolve(mixed, tap_ref)
        carry(mixed)
        aa[tile_rows(t), at * channels : (at + 1) * channels] = (middle * conv).astype(BF16)

    n1_core.wait_recv()
    for item in n1_stores:
        item.start()
    mbuf[0:EDGE, :] = jnp.zeros((EDGE, channels), F32)

    @pl.loop(0, seq_tiles)
    def _(t):
        mixer_tile(wmix, taps, 0, t)

        @pl.when(t + 1 < far)
        def _():
            gather_hop(t + 1)

    assert seq_tiles + 1 >= far
    gather_last()
    taps_copy.wait_recv()
    mbuf[0:EDGE, :] = jnp.zeros((EDGE, channels), F32)

    @pl.loop(0, seq_tiles)
    def _(t):
        mixer_tile(gm, taps2, 1, t)

    outw_copy.wait_recv()

    def branch(c, t):
        rows = pl.ds(pl.multiple_of(c * own + t * TILE, TILE), TILE)
        return dot(aa[rows, 0:channels], outw[...], 1, 0) + dot(
            aa[rows, channels : 2 * channels], outw_far[...], 1, 0
        )

    @pl.loop(0, per_block)
    def _(t):
        xr[pl.ds(pl.multiple_of(t * TILE, TILE), TILE), :] = branch(theirs, t).astype(BF16)
        branch_sum(t).start()

    @pl.loop(0, per_block)
    def _(t):
        f1[pl.ds(pl.multiple_of(t * TILE, TILE), TILE), :] = branch(mine, t)

    first_row = rows_at(0, mine)

    def own_rows(rows):
        return pl.ds(pl.multiple_of(first_row + rows.start, STRIP), STRIP)

    def second_norm(rows):
        hidden = ra[1, rows].astype(F32) + f1[rows] + ra[0, rows].astype(F32)
        f2[rows] = hidden
        acts[0, own_rows(rows)] = (hidden * rms_scale(hidden) * gain2[...]).astype(BF16)

    for t in range(per_block):
        branch_sum(t).wait()

        @pl.loop(0, TILE // STRIP)
        def _(i):
            second_norm(pl.ds(pl.multiple_of(t * TILE + i * STRIP, STRIP), STRIP))

        n2_across[t].start()
    n2_core.start()
    cot_across.wait_recv()
    cot_pass.start()

    def forward_tile(c, start):
        rows = pl.ds(pl.multiple_of(start, TILE), TILE)
        at = pl.multiple_of(c * chunk, chunk)
        both = pl.multiple_of(2 * c * chunk, chunk)
        pre = dot(acts[0, rows], wgu[pl.ds(both, 2 * chunk)], 1, 1)
        grad_activ = dot(acts[1, rows], wd[pl.ds(at, chunk)], 1, 1)
        gate_pre, up_pre = pre[:, :chunk], pre[:, chunk:]
        squash = 0.5 + 0.5 * jnp.tanh(0.5 * gate_pre)
        silu = gate_pre * squash
        aa[rows, pl.ds(at, chunk)] = (silu * up_pre).astype(BF16)
        slope = squash + silu - silu * squash
        agu[rows, pl.ds(both, chunk)] = (grad_activ * up_pre * slope).astype(BF16)
        agu[rows, pl.ds(both + chunk, chunk)] = (grad_activ * silu).astype(BF16)

    def weight_grad(c, part, rows):
        if part < 2:
            cols = pl.ds(pl.multiple_of((2 * c + part) * chunk, chunk), chunk)
            return dot(agu[rows, cols], acts[0, rows], 0, 0)
        return dot(aa[rows, pl.ds(pl.multiple_of(c * chunk, chunk), chunk)], acts[1, rows], 0, 0)

    def weight_grads(c, rows, add):
        def store(into, total):
            if add:
                total = gf[c, into, :].astype(F32) + total
            gf[c, into, :] = total.astype(BF16)

        @pl.loop(0, 2)
        def _(part):
            into = pl.ds(pl.multiple_of(part * chunk, chunk), chunk)
            cols = pl.ds(pl.multiple_of((2 * c + part) * chunk, chunk), chunk)
            store(into, dot(agu[rows, cols], acts[0, rows], 0, 0))

        cols = pl.ds(c * chunk, chunk)
        store(pl.ds(2 * chunk, chunk), dot(aa[rows, cols], acts[1, rows], 0, 0))

    def tile_list(tiles, before):
        def pick(index, at):
            value = jnp.int32(tiles[0][index])
            for i, tile in enumerate(tiles):
                value = jnp.where(at == i, jnp.int32(tile[index]), value)
            return value

        @pl.loop(0, len(tiles))
        def _(at):
            for i, wait in before.items():
                pl.when(at == i)(wait)
            c, r, other, t = (pick(index, at) for index in range(4))
            at_core = mine + other * (theirs - mine)
            forward_tile(c, rows_at(r, at_core) + t * TILE)

    def ready(*items):
        def wait():
            for item in items:
                item.wait()

        return wait

    def near_partner():
        n2_core.wait_recv()
        cot_core.wait_recv()

    def far_own(t):
        def wait():
            n2_across[t].wait_recv()
            n2_pass[t].start()

        return wait

    def far_partner(t):
        def wait():
            n2_pass[t].wait_recv()
            if t == 0:
                cot_pass.wait_recv()

        return wait

    def whole_block(c, r, other):
        return [(c, r, other, t) for t in range(per_block)]

    tile_list(
        whole_block(0, 0, 0) + whole_block(0, 0, 1),
        {0: ready(*weight_loads(0)), per_block: near_partner},
    )
    near, distant = pl.ds(0, 2 * own), pl.ds(2 * own, 2 * own)
    weight_grads(0, near, False)
    order, before = [], {}
    fillers = whole_block(1, 0, 0) + whole_block(1, 0, 1) + whole_block(2, 0, 0)
    fill = len(fillers) // (2 * per_block - 1)
    before[0] = ready(*weight_loads(1))
    for other, t in ((0, 0), (1, 0)) + tuple((o, t) for t in range(1, per_block) for o in (0, 1)):
        taken = fillers[:fill]
        fillers = fillers[fill:]
        for tile in taken:
            if tile[0] == 2 and not any(held[0] == 2 for held in order):
                before[len(order)] = ready(*weight_loads(2))
            order.append(tile)
        before[len(order)] = (far_partner if other else far_own)(t)
        order.append((0, 1, other, t))
    tile_list(order, before)
    n1_across.start()
    weight_grads(0, distant, True)
    sum_start(0)

    def far_tiles(*blocks):
        for block in blocks:
            tile_list(whole_block(*block), {})
            pump()

    def chunk_grads(c):
        weight_grads(c, pl.ds(0, group), False)
        pump()
        sum_start(c)
        pump()

    far_tiles((1, 1, 0), (1, 1, 1))
    chunk_grads(1)
    far_tiles((2, 0, 1), (2, 1, 0), (2, 1, 1))
    for copy in (
        piece_copies
        + n2_across
        + n2_pass
        + [taps_copy, outw_copy, cot_across, cot_core, cot_pass, n1_core, n1_across, n2_core]
    ):
        copy.wait_send()
    for item in n1_stores:
        item.wait()
    def gn2(rows):
        return dot(agu[rows, :], wgu[...], 1, 0)

    def to_send(r):
        def body(rows, local):
            sa[r, local] = gn2(rows).astype(BF16)

        return body

    def to_f1(rows, local):
        f1[local] = gn2(rows)

    core_copies = [mp_copy(sa.at[r], ra.at[r], partner, r) for r in range(2)]
    block_tiles(1, theirs, to_send(1))
    core_copies[1].start()
    pump()
    block_tiles(1, mine, to_f1)
    core_copies[1].wait_recv()

    def join(rows):
        ra[1, rows] = (ra[1, rows].astype(F32) + f1[rows]).astype(BF16)

    strips(join)
    across_copies = []
    for h, number in enumerate((2, base_copy + 12 + 3 * per_block)):
        rows = pl.ds(h * (own // 2), own // 2)
        across_copies.append(mp_copy(ra.at[1, rows], xr.at[rows], across, number))
        across_copies[h].start()
    pump()
    chunk_grads(2)
    pl.semaphore_signal(credit.at[2], inc=1, device_id=across, device_id_type=MESH)
    block_tiles(0, theirs, to_send(0))
    core_copies[0].start()
    pump()
    block_tiles(0, mine, to_f1)
    pump()
    n1_across.wait_recv()
    n1_pass.start()

    pump()
    n1_pass.wait()
    n1_load.start()
    n1_move.start()
    core_copies[0].wait_recv()
    smv[...] = jnp.zeros_like(smv)

    def hidden_grad(rows):
        grad = f1[rows] + ra[0, rows].astype(F32) + xr[rows].astype(F32)
        hidden = f2[rows]
        scale = rms_scale(hidden)
        smv[1:2, :] += jnp.sum(grad * hidden * scale, axis=0, keepdims=True)
        total = acts[1, own_rows(rows)].astype(F32) + rms_back(grad * gain2[...], hidden, scale)
        f1[rows] = total
        acts[1, own_rows(rows)] = total.astype(BF16)

    def block_ref(r, c, h):
        return acts.at[1, pl.ds(pl.multiple_of(rows_at(r, c) + h * (own // 2), STRIP), own // 2)]

    def branch_copy(source, target, device, number):
        return [
            mp_copy(block_ref(*source, h), block_ref(*target, h), device, number[h])
            for h in range(2)
        ]

    more = base_copy + 13 + 3 * per_block
    branch_across = branch_copy((0, mine), (1, mine), across, (3, more))
    branch_core = branch_copy((0, mine), (0, mine), partner, (4, more + 1))
    branch_pass = branch_copy((1, mine), (1, mine), partner, (5, more + 2))
    for h in range(2):
        if h == 1:
            pump()
        across_copies[h].wait_recv()

        @pl.loop(h * (own // 2 // STRIP), (h + 1) * (own // 2 // STRIP))
        def _(t):
            hidden_grad(pl.ds(pl.multiple_of(t * STRIP, STRIP), STRIP))

        if h == 1:
            for copy in core_copies + across_copies:
                copy.wait_send()
        if h == 0:
            pl.semaphore_wait(credit.at[2], 1)
        branch_across[h].start()
        branch_core[h].start()
    pump()

    def out_block(r, c, slot):
        def body(rows, local):
            to = pl.ds(pl.multiple_of(slot * own + local.start, TILE), TILE)
            agu[to, 0:width] = dot(aa[rows, :], wd[...], 1, 0).astype(BF16)

        block_tiles(r, c, body)

    for slot, (r, c) in enumerate(((1, theirs), (0, theirs), (1, mine), (0, mine))):
        out_block(r, c, slot)
        pump()

    for copy in branch_core:
        copy.wait_recv()

    out_copies = [
        mp_copy(agu.at[pl.ds((1 - r) * own, own), pl.ds(0, width)], ra.at[r], partner, 6 + r)
        for r in range(2)
    ]
    for r in (1, 0):
        out_copies[r].start()
    n1_load.wait()
    n1_move.wait()

    def mixer(r):
        def rows_of(t):
            return pl.ds(pl.multiple_of(2 * r * own + t * TILE, TILE), TILE)

        def finish(t):
            tap = [taps[k : k + 1, :] for k in range(3)]
            grad_mixed = (
                tap[2] * gbuf[0:TILE, :]
                + tap[1] * gbuf[1 : TILE + 1, :]
                + tap[0] * gbuf[2 : TILE + 2, :]
            )
            for k, kept in ((0, 1), (2, 0)):
                aa[rows_of(t), k * channels : (k + 1) * channels] = (
                    grad_mixed * pbuf[kept]
                ).astype(BF16)

        mbuf[0:EDGE, :] = jnp.zeros((EDGE, channels), F32)

        @pl.loop(0, seq_tiles)
        def _(t):
            rows = rows_of(t)
            left, middle, right = project(acts[0, rows], wmix)
            mixed = left * right
            conv, shifted = convolve(mixed, taps)
            aa[rows, 3 * channels : 4 * channels] = (middle * conv).astype(BF16)
            grad_mixer = dot(acts[1, rows], outw[...], 1, 1)
            aa[rows, channels : 2 * channels] = (grad_mixer * conv).astype(BF16)
            grad_conv = grad_mixer * middle
            for k, factor in enumerate(shifted):
                smv[2 + k : 3 + k, 0:channels] += jnp.sum(
                    grad_conv * factor, axis=0, keepdims=True
                )
            carry(mixed)

            @pl.when(t > 0)
            def _():
                gbuf[TILE:, :] = grad_conv[0:EDGE, :]
                finish(t - 1)

            gbuf[0:TILE, :] = grad_conv
            pbuf[0] = left
            pbuf[1] = right

        gbuf[TILE:, :] = jnp.zeros((EDGE, channels), F32)
        finish(seq_tiles - 1)

    mixer(0)
    pump()
    pump()

    branch_across[0].wait_recv()
    branch_pass[0].start()
    pump()
    branch_across[1].wait_recv()
    branch_pass[1].start()

    out_copies[1].wait_recv()

    def join_out(rows):
        kept = agu[pl.ds(pl.multiple_of(2 * own + rows.start, STRIP), STRIP), 0:width]
        ra[1, rows] = (ra[1, rows].astype(F32) + kept.astype(F32)).astype(BF16)

    strips(join_out)
    out_across = mp_copy(ra.at[1], xr, across, 8)
    out_across.start()
    pump()
    for copy in branch_pass:
        copy.wait_recv()
    mixer(1)
    pump()

    chunk_end(0)
    for device in (beside, along):
        pl.semaphore_signal(slots_free, inc=1, device_id=device, device_id_type=MESH)

    @pl.when(inside)
    def _():
        pl.semaphore_signal(slots_free, inc=1, device_id=middle, device_id_type=MESH)

    for copy in branch_across + branch_core + branch_pass:
        copy.wait_send()

    for k in range(4):
        used = acts[1] if k == 3 else acts[0]
        cols = slice(k * channels, (k + 1) * channels)
        gm[cols, :] = dot(aa[:, cols], used, 0, 0).astype(BF16)
        pump()
    tok_again.start()

    @pl.when(inside)
    def _():
        pl.semaphore_wait(slots_free, 3)

    @pl.when(jnp.logical_not(inside))
    def _():
        pl.semaphore_wait(slots_free, 2)

    sum_start(CHUNKS)

    def gn1(rows):
        return dot(aa[rows, 0 : 3 * channels], inw[...], 1, 0)

    def to_stage(r):
        def body(rows, local):
            to = pl.ds(pl.multiple_of(r * own + local.start, TILE), TILE)
            agu[to, width : 2 * width] = gn1(rows).astype(BF16)

        return body

    def to_f2(rows, local):
        f2[local] = gn1(rows)

    back_copies = [
        mp_copy(agu.at[pl.ds(r * own, own), pl.ds(width, width)], ra.at[r], partner, 9 + r)
        for r in range(2)
    ]
    for r in (1, 0):
        block_tiles(r, theirs, to_stage(r))
        pump()
    pump()

    out_copies[0].wait_recv()
    out_across.wait_recv()

    def finish_out(rows):
        kept = agu[pl.ds(pl.multiple_of(3 * own + rows.start, STRIP), STRIP), 0:width]
        total = f2[rows] + kept.astype(F32) + ra[0, rows].astype(F32) + xr[rows].astype(F32)
        sa[0, rows] = total.astype(BF16)

    strips(finish_out)
    out_store.start()
    for copy in out_copies + [out_across]:
        copy.wait_send()
    pl.semaphore_signal(credit.at[0], inc=1, device_id=partner, device_id_type=MESH)
    pl.semaphore_signal(credit.at[1], inc=1, device_id=across, device_id_type=MESH)

    pump()
    pl.semaphore_wait(credit.at[0], 1)
    pl.semaphore_wait(credit.at[1], 1)
    for r in (1, 0):
        back_copies[r].start()
    block_tiles(1, mine, to_f2)
    pump()
    pump()
    back_copies[1].wait_recv()

    def join_back(rows):
        ra[1, rows] = (ra[1, rows].astype(F32) + f2[rows]).astype(BF16)

    strips(join_back)
    back_across = mp_copy(ra.at[1], xr, across, 11)
    back_across.start()
    block_tiles(0, mine, to_f2)
    pump()
    pump()
    back_copies[0].wait_recv()
    back_across.wait_recv()

    def tokens_grad(rows):
        grad = f2[rows] + ra[0, rows].astype(F32) + xr[rows].astype(F32)
        grad = grad * own_mask(rows)
        x_rows = acts[0, rows].astype(F32)
        scale = rms_scale(x_rows)
        smv[0:1, :] += jnp.sum(grad * x_rows * scale, axis=0, keepdims=True)
        total = f1[rows] + rms_back(grad * gain1[...], x_rows, scale)
        sa[1, rows] = total.astype(BF16)

    tok_again.wait()
    strips(tokens_grad)
    tg_store.start()
    chunk_end(1)
    for copy in back_copies + [back_across]:
        copy.wait_send()

    small_core = mp_copy(smv, smb.at[0], partner, 12)
    small_core.start()
    pump()
    small_core.wait()
    smv[0:2, :] += smb[0, 0:2]
    small_across = mp_copy(smv, smb.at[1], across, 13)
    small_across.start()
    pump()
    small_across.wait()
    smv[0:2, :] += smb[1, 0:2]
    for hop, device in enumerate((beside, along, opposite)):
        swap = mp_copy(smv, smb.at[2 + hop], device, 14 + hop)
        swap.start()
        pump()
        swap.wait()
        smv[...] += smb[2 + hop]
    small_out[...] = smv[...]
    chunk_end(2)
    pump()
    assert next(sites, None) is None
    for number in range(CUT * CHUNKS, len(parts_list)):
        parts_list[number][2]()
        mixer_stores[number - CUT * CHUNKS].start()
    for item in grad_stores + mixer_stores:
        item.wait()
    out_store.wait()
    tg_store.wait()


def block_by_kernel(
    tokens,
    lengths,
    norm1_gain,
    in_weight,
    conv_weight,
    out_weight,
    norm2_gain,
    gate_weight,
    up_weight,
    down_weight,
    cotangent,
):
    count = lax.axis_size("dp")
    own, width = tokens.shape
    group = 4 * own
    channels = out_weight.shape[0]
    units = gate_weight.shape[0]
    chunk = units // CHUNKS
    part_rows, first = 3 * chunk // CUT, 5 * width // 8
    mp_copies = 14 + count - 1 + 16 + 3 * (own // TILE)
    anywhere = pl.BlockSpec(memory_space=pl.ANY)
    inside = pl.BlockSpec(memory_space=pltpu.VMEM)
    macs = group * width * (3 * 3 * units + 15 * channels)
    outs = pl.pallas_call(
        functools.partial(block_kernel, count),
        out_shape=(
            jax.ShapeDtypeStruct((own, width), BF16),
            jax.ShapeDtypeStruct((own, width), BF16),
            jax.ShapeDtypeStruct((units, width), BF16),
            jax.ShapeDtypeStruct((units, width), BF16),
            jax.ShapeDtypeStruct((units, width), BF16),
            jax.ShapeDtypeStruct((3 * channels, width), BF16),
            jax.ShapeDtypeStruct((channels, width), BF16),
            jax.ShapeDtypeStruct((8, width), F32),
            jax.ShapeDtypeStruct((2 * own, width), BF16),
        ),
        in_specs=[anywhere] * 7 + [inside] * 3 + [pl.BlockSpec(memory_space=pltpu.SMEM)],
        out_specs=(anywhere,) * 7 + (inside, anywhere),
        scratch_shapes=[
            pltpu.VMEM((2, group, width), BF16),
            pltpu.VMEM((2 * units, width), BF16),
            pltpu.VMEM((units, width), BF16),
            pltpu.VMEM((group, 2 * units), BF16),
            pltpu.VMEM((group, units), BF16),
            pltpu.VMEM((CHUNKS, 3 * chunk, width), BF16),
            pltpu.VMEM((CUT * CHUNKS, part_rows // 2, first), BF16),
            pltpu.VMEM((CUT * CHUNKS, 2, part_rows // 4, first), BF16),
            pltpu.VMEM((CUT * CHUNKS, 2, part_rows // 2, width - first), BF16),
            pltpu.VMEM((4 * channels, width), BF16),
            pltpu.VMEM((2, own, width), BF16),
            pltpu.VMEM((2, own, width), BF16),
            pltpu.VMEM((own, width), BF16),
            pltpu.VMEM((4 * channels, width), BF16),
            pltpu.VMEM((own, width), F32),
            pltpu.VMEM((own, width), F32),
            pltpu.VMEM((8, channels), F32),
            pltpu.VMEM((8, channels), F32),
            pltpu.VMEM((EDGE + TILE, channels), F32),
            pltpu.VMEM((TILE + EDGE, channels), F32),
            pltpu.VMEM((2, TILE, channels), F32),
            pltpu.VMEM((8, width), F32),
            pltpu.VMEM((5, 8, width), F32),
            pltpu.SemaphoreType.DMA((3 * CHUNKS + 10 + 3 * CHUNKS + SLABS,)),
            pltpu.SemaphoreType.DMA((2, 2, count // 2)),
            pltpu.SemaphoreType.DMA((2, 2, count // 2)),
            pltpu.SemaphoreType.DMA((CUT * CHUNKS + SLABS, 11)),
            pltpu.SemaphoreType.DMA((CUT * CHUNKS + SLABS, 11)),
            pltpu.SemaphoreType.REGULAR((CUT * CHUNKS + SLABS,)),
            pltpu.SemaphoreType.REGULAR((CUT * CHUNKS + SLABS,)),
            pltpu.SemaphoreType.REGULAR,
            pltpu.SemaphoreType.DMA((mp_copies,)),
            pltpu.SemaphoreType.DMA((mp_copies,)),
            pltpu.SemaphoreType.REGULAR((3,)),
        ],
        compiler_params=pltpu.CompilerParams(
            collective_id=0, has_side_effects=True, vmem_limit_bytes=VMEM_BYTES
        ),
        cost_estimate=pl.CostEstimate(
            flops=2 * macs, bytes_accessed=64 * 2**20, transcendentals=group * units
        ),
        name="block",
    )(
        tokens,
        cotangent,
        gate_weight,
        up_weight,
        down_weight,
        in_weight.reshape(3 * channels, width),
        out_weight,
        conv_weight,
        norm1_gain.reshape(1, width),
        norm2_gain.reshape(1, width),
        lengths,
    )
    held = 2 * own + 3 * units + 4 * channels
    finals = pl.pallas_call(
        widen_kernel,
        out_shape=(
            jax.ShapeDtypeStruct((own, width), BF16),
            jax.ShapeDtypeStruct((own, width), BF16),
            jax.ShapeDtypeStruct((units, width), F32),
            jax.ShapeDtypeStruct((units, width), F32),
            jax.ShapeDtypeStruct((units, width), F32),
            jax.ShapeDtypeStruct((3 * channels, width), F32),
            jax.ShapeDtypeStruct((channels, width), F32),
            jax.ShapeDtypeStruct((1, width), F32),
            jax.ShapeDtypeStruct((1, width), F32),
            jax.ShapeDtypeStruct((3, channels), F32),
        ),
        in_specs=[anywhere] * 7 + [inside],
        out_specs=(anywhere,) * 7 + (inside,) * 3,
        scratch_shapes=[
            pltpu.VMEM((held, width), BF16),
            pltpu.VMEM((held, width), F32),
            pltpu.SemaphoreType.DMA((2 * held // LANES,)),
        ],
        compiler_params=pltpu.CompilerParams(vmem_limit_bytes=WIDEN_BYTES),
        cost_estimate=pl.CostEstimate(flops=0, bytes_accessed=32 * 2**20, transcendentals=0),
        name="widen",
    )(*outs[:8])
    result, grad_tokens, gate_grad, up_grad, down_grad, in_grad, out_grad, one, two, taps = finals
    return (
        result,
        grad_tokens,
        one.reshape(width),
        in_grad.reshape(3, channels, width),
        taps,
        out_grad,
        two.reshape(width),
        gate_grad,
        up_grad,
        down_grad,
    )


def widen_kernel(*refs):
    sources, small = refs[:7], refs[7]
    targets, one, two, taps = refs[8:15], refs[15], refs[16], refs[17]
    narrow, wide, sem = refs[18:]
    moves = []
    at = 0
    for i, (source, target) in enumerate(zip(sources, targets)):
        rows = source.shape[0]
        if rows % WIDEN_ROWS == 0:
            rows = WIDEN_ROWS
        for row in range(0, source.shape[0], rows):
            place, held = pl.ds(row, rows), pl.ds(at, rows)
            number = 2 * len(moves)
            read = pltpu.make_async_copy(source.at[place], narrow.at[held], sem.at[number])
            out = (narrow if i < 2 else wide).at[held]
            write = pltpu.make_async_copy(out, target.at[place], sem.at[number + 1])
            read.start()
            moves.append((read, write, held, i >= 2))
            at += rows
    one[...] = small[0:1, :]
    two[...] = small[1:2, :]
    taps[...] = small[2:5, : taps.shape[1]]
    for read, write, held, widens in moves:
        read.wait()
        if widens:
            wide[held, :] = narrow[held, :].astype(F32)
        write.start()
    for _, write, _, _ in moves:
        write.wait()


VMEM_BYTES = 62 * 2**20
WIDEN_BYTES = 62 * 2**20
WIDEN_ROWS = 384


def on_device(
    tokens,
    lengths,
    norm1_gain,
    in_weight,
    conv_weight,
    out_weight,
    norm2_gain,
    gate_weight,
    up_weight,
    down_weight,
    cotangent,
):
    assert 2 * tokens.shape[0] == SEQ_LEN
    fits = lax.axis_size("mp") == 4 and lax.axis_size("dp") == 8
    block = block_by_kernel if fits else block_by_ops
    return block(
        tokens,
        lengths,
        norm1_gain,
        in_weight,
        conv_weight,
        out_weight,
        norm2_gain,
        gate_weight,
        up_weight,
        down_weight,
        cotangent,
    )


def solution(mesh):
    rows = P(("dp", "mp"), None)
    hidden_rows = P("mp", None)
    placed = (
        rows,
        P("dp"),
        P(),
        P(None, "mp", None),
        P(None, "mp"),
        hidden_rows,
        P(),
        hidden_rows,
        hidden_rows,
        hidden_rows,
        rows,
    )
    return jax.shard_map(
        on_device,
        mesh=mesh,
        in_specs=placed,
        out_specs=(
            rows,
            rows,
            P(),
            P(None, "mp", None),
            P(None, "mp"),
            hidden_rows,
            P(),
            hidden_rows,
            hidden_rows,
            hidden_rows,
        ),
        check_vma=False,
    )
```
